32 devices in a mesh: tm: 4 (over x, core), fsdp: 8 (over z, y).
Axes of the slice: x: 2, y: 2, z: 4, core: 2. Of those that a mesh axis runs over, the one named last changes fastest.
Arguments:
- frames: bfloat16 [8, 2048, 512], P('fsdp', 'tm'), may hold values from -12 to 12
- retention: float32 [8, 2048, 512], P('fsdp', 'tm'), may hold values from 0.4 to 1
- first_conv: bfloat16 [1024, 1024], P('fsdp'), may hold values from -0.1875 to 0.1875
- second_conv: bfloat16 [1024, 1024], P('fsdp'), may hold values from -0.1875 to 0.1875
- cotangent: bfloat16 [8, 2048, 512], P('fsdp', 'tm'), may hold values from -0.125 to 0.125
Outputs:
- top_hidden: bfloat16 [8, 2048, 512], P('fsdp', 'tm')
- grad_first: float32 [1024, 1024], P('fsdp')
- grad_second: float32 [1024, 1024], P('fsdp')
The draws below stay inside these ranges and needn't reach their ends.
All inputs are finite; a program needn't handle non-finite values.
Results may differ from the reference program's by a relative error of at most 0.035.
Values may be sent and summed in bfloat16 or wider, within the bound.
A program may use at most 128 MiB of HBM per device.

```python
import math
import jax
import jax.numpy as jnp
from jax import lax

RESIDUAL_WIDTH = 512
FRAMES_DEV = 512
SHORT_SPACING = 128
LONG_SPACING = 512
TRACE_DURATION = 2048
TRACE_TOTAL = 8


def draw_frames(key, part):
    stochastic_seeds = jax.random.split(jax.random.fold_in(key, 11), 3)
    levels = 1.5 * jax.random.normal(stochastic_seeds[0], (TRACE_TOTAL, 1, RESIDUAL_WIDTH), jnp.float32)
    jitter = jax.random.normal(stochastic_seeds[1], (TRACE_TOTAL, TRACE_DURATION, RESIDUAL_WIDTH), jnp.float32)
    pairing = jax.random.permutation(stochastic_seeds[2], TRACE_TOTAL)
    owner_block = jnp.arange(RESIDUAL_WIDTH) * TRACE_TOTAL // RESIDUAL_WIDTH
    spike_gain = jnp.where(owner_block[None, :] == pairing[:, None], 3.0, 1.0)[:, None, :]
    payload_elements = (levels + jitter) * spike_gain
    return jnp.clip(payload_elements, -12.0, 12.0).astype(jnp.bfloat16)


def draw_retention(key, part):
    stochastic_seeds = jax.random.split(jax.random.fold_in(key, 23), 6)
    quick_share = 0.5
    fast_selector = jax.random.bernoulli(stochastic_seeds[0], quick_share, (TRACE_TOTAL, 1, RESIDUAL_WIDTH))
    fast_frequencies = jnp.exp(jax.random.uniform(stochastic_seeds[1], (TRACE_TOTAL, 1, RESIDUAL_WIDTH), jnp.float32, math.log(1.0 / 50.0), math.log(1.0 / 30.0)))
    gradual_frequencies = jax.random.uniform(stochastic_seeds[2], (TRACE_TOTAL, 1, RESIDUAL_WIDTH), jnp.float32, 0.15, 0.5) / TRACE_DURATION
    spike_frequencies = jnp.where(fast_selector, fast_frequencies, gradual_frequencies)
    group_scale = jnp.exp(jax.random.uniform(stochastic_seeds[3], (TRACE_TOTAL, TRACE_DURATION // FRAMES_DEV, 1), jnp.float32, math.log(0.5), math.log(2.0)))
    group_scale = jnp.repeat(group_scale, FRAMES_DEV, axis=1)
    spell_locus = jax.random.randint(stochastic_seeds[4], (TRACE_TOTAL, 1, 3), 0, TRACE_DURATION)
    timestep_number = jnp.arange(TRACE_DURATION)[None, :, None]
    spell_on = jnp.any(timestep_number == spell_locus, axis=2)[:, :, None]
    spell_persistence = jax.random.uniform(stochastic_seeds[5], (TRACE_TOTAL, TRACE_DURATION, 1), jnp.float32, 0.5, 0.8)
    payload_elements = jnp.exp(-spike_frequencies * group_scale) * jnp.where(spell_on, spell_persistence, 1.0)
    return payload_elements.astype(jnp.float32)


def level_of(key, shape, shards, least, largest):
    def one(dim, blocks):
        steps = jax.random.uniform(jax.random.fold_in(jax.random.fold_in(key, 6), dim), (blocks,), jnp.float32, least / len(shards), largest / len(shards))
        return jnp.repeat(jnp.exp(steps), shape[dim] // blocks).reshape((-1,) + (1,) * (len(shape) - dim - 1))

    factor_of = one(*shards[0])
    for cut in shards[1:]:
        factor_of = factor_of * one(*cut)
    return factor_of


def scatter_about(stream_key, dims, deviation, most, cuts=(), held_as=jnp.bfloat16):
    array = deviation * jax.random.normal(stream_key, dims, jnp.float32)
    if cuts:
        array = array * level_of(stream_key, dims, cuts, -0.22, 0.18)
    return jnp.clip(array, -most, most).astype(held_as)


def setup_inputs(seed: int = 0) -> dict:
    seeds = jax.random.split(jax.random.key(seed), 6)
    return {
        "frames": draw_frames(jax.random.fold_in(seeds[5], 71), 0),
        "retention": draw_retention(jax.random.fold_in(seeds[5], 71), 0),
        "first_conv": scatter_about(seeds[2], (2 * RESIDUAL_WIDTH, 2 * RESIDUAL_WIDTH), (2 * RESIDUAL_WIDTH) ** -0.5, 0.1875, ((0, 8),)),
        "second_conv": scatter_about(seeds[3], (2 * RESIDUAL_WIDTH, 2 * RESIDUAL_WIDTH), (2 * RESIDUAL_WIDTH) ** -0.5, 0.1875, ((0, 8),)),
        "cotangent": scatter_about(seeds[4], (TRACE_TOTAL, TRACE_DURATION, RESIDUAL_WIDTH), ((TRACE_TOTAL * TRACE_DURATION) ** -0.5), 0.125, ((0, 8), (1, 4))),
    }


def combine_maps(earlier, later):
    return (earlier[0] * later[0], later[0] * earlier[1] + later[1])

def gated(pre_values):
    split_at = pre_values.shape[1] // 2
    return jnp.tanh(pre_values[:, :split_at]) * jax.nn.sigmoid(pre_values[:, split_at:])

def gate_grad(pre_values, incoming_gradient):
    split_at = pre_values.shape[1] // 2
    tanh_part = jnp.tanh(pre_values[:, :split_at])
    gate_part = jax.nn.sigmoid(pre_values[:, split_at:])
    return jnp.concatenate([incoming_gradient * gate_part * (1.0 - tanh_part * tanh_part), incoming_gradient * tanh_part * gate_part * (1.0 - gate_part)], axis=1)

def lagged_input(payload_elements, shift_by):
    return jnp.concatenate([jnp.zeros((shift_by, payload_elements.shape[1]), payload_elements.dtype), payload_elements[:payload_elements.shape[0] - shift_by]], axis=0)

def shifted_ahead(payload_elements, shift_by):
    return jnp.concatenate([payload_elements[shift_by:], jnp.zeros((shift_by, payload_elements.shape[1]), payload_elements.dtype)], axis=0)

def block_sums(operand, gradients):
    blocks = operand.shape[0] // FRAMES_DEV
    left_side = operand.reshape(blocks, FRAMES_DEV, operand.shape[1]).astype(jnp.float32)
    right_side = gradients.reshape(blocks, FRAMES_DEV, gradients.shape[1]).astype(jnp.float32)
    partials = jnp.einsum('kti,ktj->kij', left_side, right_side)
    rounded = lax.optimization_barrier(partials.astype(jnp.bfloat16))
    return lax.optimization_barrier(jnp.sum(rounded.astype(jnp.float32), axis=0))

def reference(frames, retention, first_conv, second_conv, cotangent):

    def one_sequence(totals, inputs):
        sequence, keep_rate, upstream_in = inputs
        payload_elements = sequence.astype(jnp.float32)
        factor, baseline = lax.associative_scan(combine_maps, (keep_rate, (1.0 - keep_rate) * payload_elements), axis=0)
        trend_removed = (payload_elements - baseline).astype(jnp.bfloat16)
        opening_layer_input = jnp.concatenate([lagged_input(trend_removed, SHORT_SPACING), trend_removed], axis=1)
        first_pre = jnp.dot(opening_layer_input, first_conv, preferred_element_type=jnp.float32)
        opening_layer_output = (trend_removed.astype(jnp.float32) + gated(first_pre)).astype(jnp.bfloat16)
        closing_layer_input = jnp.concatenate([lagged_input(opening_layer_output, LONG_SPACING), opening_layer_output], axis=1)
        second_pre = jnp.dot(closing_layer_input, second_conv, preferred_element_type=jnp.float32)
        top_hidden = (opening_layer_output.astype(jnp.float32) + gated(second_pre)).astype(jnp.bfloat16)
        incoming_gradient = upstream_in.astype(jnp.float32)
        second_grad = gate_grad(second_pre, incoming_gradient).astype(jnp.bfloat16)
        closing_backward = jnp.dot(second_grad, second_conv.T, preferred_element_type=jnp.float32)
        opening_upstream_gradient = incoming_gradient + closing_backward[:, RESIDUAL_WIDTH:] + shifted_ahead(closing_backward[:, :RESIDUAL_WIDTH], LONG_SPACING)
        first_grad = gate_grad(first_pre, opening_upstream_gradient).astype(jnp.bfloat16)
        new_totals = (totals[0] + block_sums(opening_layer_input, first_grad), totals[1] + block_sums(closing_layer_input, second_grad))
        return (new_totals, top_hidden)
    empty = jnp.zeros((2 * RESIDUAL_WIDTH, 2 * RESIDUAL_WIDTH), jnp.float32)
    totals, top_hidden = lax.scan(one_sequence, (empty, empty), (frames, retention, cotangent))
    return (top_hidden, totals[0], totals[1])
```

```python
import jax
import jax.numpy as jnp
from jax import lax
from jax.experimental import pallas as pl
from jax.experimental.pallas import tpu as pltpu
from jax.sharding import PartitionSpec as P

MESH = pl.DeviceIdType.MESH
F32 = jnp.float32
BF16 = jnp.bfloat16
SEGS = 8


def prefix(part, axis, combine, identity):
    place = lax.axis_index(axis)
    gathered = jax.tree.map(lambda a: lax.all_gather(a, axis), part)
    state = jax.tree.map(lambda a, e: jnp.zeros_like(a) + jnp.asarray(e, a.dtype), part, identity)

    def one(step, state):
        return combine(
            state, jax.tree.map(lambda a: lax.dynamic_index_in_dim(a, step, 0, False), gathered)
        )

    return lax.fori_loop(0, place, one, state)


def passed_along(value, axis, steps):
    count = lax.axis_size(axis)
    leading, last = (max(0, -steps), min(count, count - steps))
    return lax.ppermute(value, axis, [(source, source + steps) for source in range(leading, last)])


def combine_maps(earlier, later):
    return (earlier[0] * later[0], later[0] * earlier[1] + later[1])


def gated(pre_values):
    split_at = pre_values.shape[1] // 2
    return jnp.tanh(pre_values[:, :split_at]) * jax.nn.sigmoid(pre_values[:, split_at:])


def gate_grad(pre_values, incoming_gradient):
    split_at = pre_values.shape[1] // 2
    tanh_part = jnp.tanh(pre_values[:, :split_at])
    gate_part = jax.nn.sigmoid(pre_values[:, split_at:])
    return jnp.concatenate(
        [
            incoming_gradient * gate_part * (1.0 - tanh_part * tanh_part),
            incoming_gradient * tanh_part * gate_part * (1.0 - gate_part),
        ],
        axis=1,
    )


def accumulate_with(operand, weights_block):
    return jnp.dot(operand, weights_block, preferred_element_type=jnp.float32)


def back_with(gradients, weights_block):
    return lax.dot_general(
        gradients, weights_block, (((1,), (1,)), ((), ())), preferred_element_type=jnp.float32
    )


def weight_term(operand, gradients):
    return lax.dot_general(
        operand, gradients, (((0,), (0,)), ((), ())), preferred_element_type=jnp.float32
    )


def on_device(frames, retention, first_conv, second_conv, cotangent):
    payload_elements = frames[0].astype(jnp.float32)
    keep_rate = retention[0]
    length, channels = payload_elements.shape
    short_lag = length // 4
    factor, local_part = lax.associative_scan(
        combine_maps, (keep_rate, (1.0 - keep_rate) * payload_elements), axis=0
    )
    identity_map = (jnp.ones((channels,), jnp.float32), jnp.zeros((channels,), jnp.float32))
    carried_in = prefix((factor[-1], local_part[-1]), "tm", combine_maps, identity_map)
    trend_removed = (payload_elements - (local_part + factor * carried_in[1][None, :])).astype(
        jnp.bfloat16
    )
    tail_rows = trend_removed[length - short_lag :]
    near_tail = passed_along(tail_rows, "tm", 1)
    own_past = jnp.concatenate([near_tail, trend_removed[: length - short_lag]], axis=0)
    opening_layer_input = jnp.concatenate([own_past, trend_removed], axis=1)
    stacked_pre = accumulate_with(
        opening_layer_input, lax.all_gather(first_conv, "fsdp", axis=0, tiled=True)
    )
    stacked_out = (trend_removed.astype(jnp.float32) + gated(stacked_pre)).astype(jnp.bfloat16)
    earlier_out = passed_along(stacked_out, "tm", 1)
    closing_layer_input = jnp.concatenate([earlier_out, stacked_out], axis=1)
    second_pre = accumulate_with(
        closing_layer_input, lax.all_gather(second_conv, "fsdp", axis=0, tiled=True)
    )
    top_hidden = (stacked_out.astype(jnp.float32) + gated(second_pre)).astype(jnp.bfloat16)
    incoming_gradient = cotangent[0].astype(jnp.float32)
    second_grad = gate_grad(second_pre, incoming_gradient).astype(jnp.bfloat16)
    second_shard = lax.psum_scatter(
        weight_term(closing_layer_input, second_grad).astype(jnp.bfloat16),
        "fsdp",
        scatter_dimension=0,
        tiled=True,
    )
    grad_second = lax.psum(second_shard, "tm").astype(jnp.float32)
    closing_backward = back_with(
        second_grad, lax.all_gather(second_conv, "fsdp", axis=0, tiled=True)
    )
    carried_back = passed_along(
        closing_backward[:, :channels].astype(jnp.bfloat16), "tm", -1
    ).astype(jnp.float32)
    opening_upstream_gradient = incoming_gradient + closing_backward[:, channels:] + carried_back
    first_grad = gate_grad(stacked_pre, opening_upstream_gradient).astype(jnp.bfloat16)
    first_shard = lax.psum_scatter(
        weight_term(opening_layer_input, first_grad).astype(jnp.bfloat16),
        "fsdp",
        scatter_dimension=0,
        tiled=True,
    )
    grad_first = lax.psum(first_shard, "tm").astype(jnp.float32)
    return (top_hidden[None], grad_first, grad_second)


def sigmoid(value):
    return 0.5 * jnp.tanh(0.5 * value) + 0.5


def kernel(
    frames, keep, w1_hbm, w2_hbm, cot,
    top, grad1, grad2,
    xs, ks, hs, x1, tail_in, out1, prev_out, w1, w2,
    th1, sg1, pre2, g, cb, cb_in,
    ends, part, core_in, core_sum, x_in, x_sum, f_in, quarter,
    local_sem, gs, gr, es, er, ns, nr, ss, sr, fs_s, fs_r, qs, qr,
):
    T, F = 4, 8
    t, f = lax.axis_index("tm"), lax.axis_index("fsdp")
    x, c = t // 2, t % 2
    across = (1 - x) * 2 + c
    sibling = x * 2 + (1 - c)
    frames_n, ch = frames.shape
    seg = frames_n // SEGS
    lag = frames_n // 4
    shard = w1_hbm.shape[0]
    q = shard // T
    pending = []

    def rows(start, size):
        return pl.ds(pl.multiple_of(start, size), size)

    def send(src, dst, ssem, rsem, tm, fsdp):
        copy = pltpu.make_async_remote_copy(
            src_ref=src, dst_ref=dst, send_sem=ssem, recv_sem=rsem,
            device_id=(tm, fsdp), device_id_type=MESH,
        )
        copy.start()
        pending.append(copy)
        return copy

    own = [
        pltpu.make_async_copy(wh, w.at[rows(f * shard, shard), :], local_sem.at[m])
        for m, (wh, w) in enumerate(((w1_hbm, w1), (w2_hbm, w2)))
    ]
    for copy in own:
        copy.start()

    barrier = pltpu.get_barrier_semaphore()
    for k in range(1, F):
        pl.semaphore_signal(
            barrier, inc=1, device_id=(t, lax.rem(f + k, F)), device_id_type=MESH
        )
    for k in range(1, T):
        pl.semaphore_signal(
            barrier, inc=1, device_id=(lax.rem(t + k, T), f), device_id_type=MESH
        )
    pl.semaphore_wait(barrier, F + T - 2)

    def piece(w, owner, place):
        return w.at[rows(owner * shard + place * q, q), :]

    spread = [[], []]
    for m, (wh, w) in enumerate(((w1_hbm, w1), (w2_hbm, w2))):
        for k in range(1, F):
            spread[m].append(
                send(wh.at[rows(t * q, q), :], piece(w, f, t),
                     gs.at[m, 0, k], gr.at[m, 0, k], t, lax.rem(f + k, F))
            )

    def complete(m, w):
        over_x, over_core = [], []
        for k in range(1, F):
            owner = lax.rem(f + F - k, F)
            spread[m][k - 1].wait_recv()
            mine = piece(w, owner, t)
            over_x.append(send(mine, mine, gs.at[m, 1, k], gr.at[m, 1, k], across, f))
            over_core.append(send(mine, mine, gs.at[m, 2, k], gr.at[m, 2, k], sibling, f))
        for k in range(1, F):
            owner = lax.rem(f + F - k, F)
            over_x[k - 1].wait_recv()
            mine = piece(w, owner, across)
            over_core.append(send(mine, mine, gs.at[m, 3, k], gr.at[m, 3, k], sibling, f))
        for copy in over_core:
            copy.wait_recv()
        own[m].wait()

    lanes = xs.shape[2]
    groups = ch // lanes

    @pl.loop(0, frames_n, step=64)
    def _(r):
        at = rows(r, 64)
        for j in range(groups):
            cols = pl.ds(j * lanes, lanes)
            xs[j, at, :] = frames[at, cols].astype(F32)
            ks[j, at, :] = keep[at, cols]

    def step(i, state):
        at = pl.ds(i, SEGS, stride=seg)
        new = []
        for j, (h, p) in enumerate(state):
            a = ks[j, at, :]
            h = a * h + (1.0 - a) * xs[j, at, :]
            p = p * a
            hs[j, at, :] = h
            ks[j, at, :] = p
            new.append((h, p))
        return tuple(new)

    nought = (jnp.zeros((SEGS, lanes), F32), jnp.ones((SEGS, lanes), F32))
    lax.fori_loop(0, seg, step, (nought,) * groups, unroll=4)
    before = []
    for j in range(groups):
        p, h = jnp.ones((1, lanes), F32), jnp.zeros((1, lanes), F32)
        before.append([])
        for s in range(SEGS):
            before[j].append((p, h))
            last = pl.ds((s + 1) * seg - 1, 1)
            p, h = ks[j, last, :] * p, ks[j, last, :] * h + hs[j, last, :]
        cols = pl.ds(j * lanes, lanes)
        ends[t, 0:8, cols] = jnp.broadcast_to(p, (8, lanes))
        ends[t, 8:16, cols] = jnp.broadcast_to(h, (8, lanes))
    states = [
        send(ends.at[t], ends.at[t], es.at[k], er.at[k], lax.rem(t + k, T), f)
        for k in range(1, T)
    ]
    for copy in states:
        copy.wait_recv()
    carried = jnp.zeros((1, ch), F32)
    for j in range(T):
        pj = ends[j, 0:1, :]
        hj = ends[j, 8:9, :]
        carried = jnp.where(j < t, pj * carried + hj, carried)
    for j in range(groups):
        cols = slice(j * lanes, (j + 1) * lanes)
        for s in range(SEGS):
            pb, hb = before[j][s]
            start = hb + pb * carried[:, cols]
            at = pl.ds(s * seg, seg)
            x1[at, ch + j * lanes : ch + (j + 1) * lanes] = (
                xs[j, at, :] - (hs[j, at, :] + ks[j, at, :] * start)
            ).astype(BF16)

    def neighbour(src, dst, n, tm):
        return pltpu.make_async_remote_copy(
            src_ref=src, dst_ref=dst, send_sem=ns.at[n], recv_sem=nr.at[n],
            device_id=(tm, f), device_id_type=MESH,
        )

    nxt, prv = lax.rem(t + 1, T), lax.rem(t + T - 1, T)
    has_next, has_prev = t < T - 1, t > 0

    tail = neighbour(x1.at[pl.ds(frames_n - lag, lag), pl.ds(ch, ch)], tail_in, 0, nxt)
    pl.when(has_next)(tail.start)
    x1[lag:, :ch] = x1[: frames_n - lag, ch:]

    complete(0, w1)

    @pl.when(has_prev)
    def _():
        tail.wait_recv()
        x1[:lag, :ch] = tail_in[...]

    @pl.when(t == 0)
    def _():
        x1[:lag, :ch] = jnp.zeros((lag, ch), BF16)

    block = 128

    @pl.loop(0, frames_n, step=block)
    def _(r):
        at = rows(r, block)
        pre = jnp.dot(x1[at, :], w1[...], preferred_element_type=F32)
        th, sg = jnp.tanh(pre[:, :ch]), sigmoid(pre[:, ch:])
        th1[at, :] = th
        sg1[at, :] = sg
        out1[at, :] = (x1[at, ch:].astype(F32) + th * sg).astype(BF16)

    passed = neighbour(out1, prev_out, 1, nxt)
    pl.when(has_next)(passed.start)

    complete(1, w2)

    @pl.loop(0, frames_n, step=block)
    def _(r):
        at = rows(r, block)
        pre2[at, :] = jnp.dot(out1[at, :], w2[ch:, :], preferred_element_type=F32)

    @pl.when(has_prev)
    def _():
        passed.wait_recv()

    @pl.when(t == 0)
    def _():
        prev_out[...] = jnp.zeros((frames_n, ch), BF16)

    @pl.loop(0, frames_n, step=block)
    def _(r):
        at = rows(r, block)
        pre = pre2[at, :] + jnp.dot(prev_out[at, :], w2[:ch, :], preferred_element_type=F32)
        th, sg = jnp.tanh(pre[:, :ch]), sigmoid(pre[:, ch:])
        u = cot[at, :].astype(F32)
        top[at, :] = (out1[at, :].astype(F32) + th * sg).astype(BF16)
        g2 = jnp.concatenate(
            [u * sg * (1.0 - th * th), u * th * sg * (1.0 - sg)], axis=1
        ).astype(BF16)
        g[0, at, :] = g2
        cb[at, :] = lax.dot_general(
            g2, w2[:ch, :], (((1,), (1,)), ((), ())), preferred_element_type=F32
        ).astype(BF16)

    back = neighbour(cb, cb_in, 2, prv)
    pl.when(has_prev)(back.start)

    def partial(m, left, first_owner):
        @pl.loop(0, ch // shard)
        def _(j):
            cols = pl.ds(pl.multiple_of(j * shard, shard), shard)
            product = lax.dot_general(
                left[:, cols], g[m], (((0,), (0,)), ((), ())), preferred_element_type=F32
            )
            part[m, first_owner + j] = product.astype(BF16).reshape(2, 2, q, 2 * ch)

    def core_phase(m):
        return send(part.at[m, :, :, 1 - c], core_in.at[m], ss.at[m, 0], sr.at[m, 0], sibling, f)

    def x_phase(m, copy):
        copy.wait_recv()

        @pl.loop(0, F)
        def _(j):
            core_sum[m, j] = (
                part[m, j, :, c].astype(F32) + core_in[m, j].astype(F32)
            ).astype(BF16)

        return send(core_sum.at[m, :, 1 - x], x_in.at[m], ss.at[m, 1], sr.at[m, 1], across, f)

    def f_phase(m, copy):
        copy.wait_recv()

        @pl.loop(0, F)
        def _(j):
            x_sum[m, j] = (
                core_sum[m, j, x].astype(F32) + x_in[m, j].astype(F32)
            ).astype(BF16)

        sends = []
        for k in range(1, F):
            to = lax.rem(f + k, F)
            sends.append(
                send(x_sum.at[m, to], f_in.at[m, k], fs_s.at[m, k], fs_r.at[m, k], t, to)
            )
        return sends

    def q_phase(m, sends):
        total = x_sum[m, f].astype(F32)
        for k in range(1, F):
            sends[k - 1].wait_recv()
            total += f_in[m, k].astype(F32)
        quarter[m, t] = total.astype(BF16)
        return [
            send(quarter.at[m, t], quarter.at[m, t], qs.at[m, k], qr.at[m, k],
                 lax.rem(t + k, T), f)
            for k in range(1, T)
        ]

    def finish(m, sends, grad):
        for copy in sends:
            copy.wait_recv()
        for j in range(T):
            grad[pl.ds(j * q, q), :] = quarter[m, j].astype(F32)

    half = ch // shard
    partial(0, prev_out, 0)
    partial(0, out1, half)
    core2 = core_phase(0)

    @pl.loop(0, frames_n, step=block)
    def _(r):
        at = rows(r, block)
        pre2[at, :ch] = cot[at, :].astype(F32) + lax.dot_general(
            g[0, at, :], w2[ch:, :], (((1,), (1,)), ((), ())), preferred_element_type=F32
        )

    over2 = x_phase(0, core2)

    @pl.when(has_next)
    def _():
        back.wait_recv()

    @pl.when(t == T - 1)
    def _():
        cb_in[...] = jnp.zeros((frames_n, ch), BF16)

    @pl.loop(0, frames_n, step=block)
    def _(r):
        at = rows(r, block)
        u = pre2[at, :ch] + cb_in[at, :].astype(F32)
        th, sg = th1[at, :], sg1[at, :]
        g[1, at, :] = jnp.concatenate(
            [u * sg * (1.0 - th * th), u * th * sg * (1.0 - sg)], axis=1
        ).astype(BF16)

    partial(1, x1.at[:, pl.ds(0, ch)], 0)
    partial(1, x1.at[:, pl.ds(ch, ch)], half)
    core1 = core_phase(1)
    over1 = x_phase(1, core1)
    spread2 = f_phase(0, over2)
    spread1 = f_phase(1, over1)
    last2 = q_phase(0, spread2)
    last1 = q_phase(1, spread1)
    finish(0, last2, grad2)
    finish(1, last1, grad1)

    for copy in pending:
        copy.wait_send()
    pl.when(has_next)(tail.wait_send)
    pl.when(has_next)(passed.wait_send)
    pl.when(has_prev)(back.wait_send)


def fused(frames, retention, first_conv, second_conv, cotangent):
    _, n, ch = frames.shape
    shard, wide = first_conv.shape
    T, F = 4, 8
    q = shard // T
    vm = lambda shape, dtype: pltpu.VMEM(shape, dtype)
    dma = pltpu.SemaphoreType.DMA
    vspec = pl.BlockSpec(memory_space=pltpu.VMEM)
    anyspec = pl.BlockSpec(memory_space=pl.ANY)
    top, grad1, grad2 = pl.pallas_call(
        kernel,
        out_shape=(
            jax.ShapeDtypeStruct((n, ch), BF16),
            jax.ShapeDtypeStruct((shard, wide), F32),
            jax.ShapeDtypeStruct((shard, wide), F32),
        ),
        in_specs=[vspec, vspec, anyspec, anyspec, vspec],
        out_specs=(vspec, vspec, vspec),
        scratch_shapes=[
            vm((ch // 128, n, 128), F32), vm((ch // 128, n, 128), F32), vm((ch // 128, n, 128), F32),
            vm((n, wide), BF16), vm((n // 4, ch), BF16), vm((n, ch), BF16), vm((n, ch), BF16),
            vm((wide, wide), BF16), vm((wide, wide), BF16),
            vm((n, ch), F32), vm((n, ch), F32), vm((n, wide), F32),
            vm((2, n, wide), BF16), vm((n, ch), BF16), vm((n, ch), BF16),
            vm((T, 16, ch), F32),
            vm((2, F, 2, 2, q, wide), BF16), vm((2, F, 2, q, wide), BF16),
            vm((2, F, 2, q, wide), BF16), vm((2, F, q, wide), BF16),
            vm((2, F, q, wide), BF16), vm((2, F, q, wide), BF16),
            vm((2, T, q, wide), BF16),
            dma((2,)), dma((2, 4, F)), dma((2, 4, F)), dma((T,)), dma((T,)),
            dma((3,)), dma((3,)), dma((2, 2)), dma((2, 2)),
            dma((2, F)), dma((2, F)), dma((2, T)), dma((2, T)),
        ],
        compiler_params=pltpu.CompilerParams(
            collective_id=0, has_side_effects=True, vmem_limit_bytes=56 * 2**20
        ),
        cost_estimate=pl.CostEstimate(
            flops=10 * n * wide * wide, bytes_accessed=8 * n * wide, transcendentals=2 * n * wide
        ),
    )(frames[0], retention[0], first_conv, second_conv, cotangent[0])
    return (top[None], grad1, grad2)


def solution(mesh):
    fits = mesh.shape["tm"] == 4 and mesh.shape["fsdp"] == 8
    in_specs = (
        P("fsdp", "tm", None),
        P("fsdp", "tm", None),
        P("fsdp", None),
        P("fsdp", None),
        P("fsdp", "tm", None),
    )
    out_specs = (P("fsdp", "tm", None), P("fsdp", None), P("fsdp", None))
    return jax.shard_map(
        fused if fits else on_device,
        mesh=mesh,
        in_specs=in_specs,
        out_specs=out_specs,
        check_vma=False,
    )
```

```python
import jax
import jax.numpy as jnp
from jax import lax
from jax.experimental import pallas as pl
from jax.experimental.pallas import tpu as pltpu
from jax.sharding import PartitionSpec as P

MESH = pl.DeviceIdType.MESH
F32 = jnp.float32
BF16 = jnp.bfloat16
SEGS = 8


def prefix(part, axis, combine, identity):
    place = lax.axis_index(axis)
    gathered = jax.tree.map(lambda a: lax.all_gather(a, axis), part)
    state = jax.tree.map(lambda a, e: jnp.zeros_like(a) + jnp.asarray(e, a.dtype), part, identity)

    def one(step, state):
        return combine(
            state, jax.tree.map(lambda a: lax.dynamic_index_in_dim(a, step, 0, False), gathered)
        )

    return lax.fori_loop(0, place, one, state)


def passed_along(value, axis, steps):
    count = lax.axis_size(axis)
    leading, last = (max(0, -steps), min(count, count - steps))
    return lax.ppermute(value, axis, [(source, source + steps) for source in range(leading, last)])


def combine_maps(earlier, later):
    return (earlier[0] * later[0], later[0] * earlier[1] + later[1])


def gated(pre_values):
    split_at = pre_values.shape[1] // 2
    return jnp.tanh(pre_values[:, :split_at]) * jax.nn.sigmoid(pre_values[:, split_at:])


def gate_grad(pre_values, incoming_gradient):
    split_at = pre_values.shape[1] // 2
    tanh_part = jnp.tanh(pre_values[:, :split_at])
    gate_part = jax.nn.sigmoid(pre_values[:, split_at:])
    return jnp.concatenate(
        [
            incoming_gradient * gate_part * (1.0 - tanh_part * tanh_part),
            incoming_gradient * tanh_part * gate_part * (1.0 - gate_part),
        ],
        axis=1,
    )


def accumulate_with(operand, weights_block):
    return jnp.dot(operand, weights_block, preferred_element_type=jnp.float32)


def back_with(gradients, weights_block):
    return lax.dot_general(
        gradients, weights_block, (((1,), (1,)), ((), ())), preferred_element_type=jnp.float32
    )


def weight_term(operand, gradients):
    return lax.dot_general(
        operand, gradients, (((0,), (0,)), ((), ())), preferred_element_type=jnp.float32
    )


def on_device(frames, retention, first_conv, second_conv, cotangent):
    payload_elements = frames[0].astype(jnp.float32)
    keep_rate = retention[0]
    length, channels = payload_elements.shape
    short_lag = length // 4
    factor, local_part = lax.associative_scan(
        combine_maps, (keep_rate, (1.0 - keep_rate) * payload_elements), axis=0
    )
    identity_map = (jnp.ones((channels,), jnp.float32), jnp.zeros((channels,), jnp.float32))
    carried_in = prefix((factor[-1], local_part[-1]), "tm", combine_maps, identity_map)
    trend_removed = (payload_elements - (local_part + factor * carried_in[1][None, :])).astype(
        jnp.bfloat16
    )
    tail_rows = trend_removed[length - short_lag :]
    near_tail = passed_along(tail_rows, "tm", 1)
    own_past = jnp.concatenate([near_tail, trend_removed[: length - short_lag]], axis=0)
    opening_layer_input = jnp.concatenate([own_past, trend_removed], axis=1)
    stacked_pre = accumulate_with(
        opening_layer_input, lax.all_gather(first_conv, "fsdp", axis=0, tiled=True)
    )
    stacked_out = (trend_removed.astype(jnp.float32) + gated(stacked_pre)).astype(jnp.bfloat16)
    earlier_out = passed_along(stacked_out, "tm", 1)
    closing_layer_input = jnp.concatenate([earlier_out, stacked_out], axis=1)
    second_pre = accumulate_with(
        closing_layer_input, lax.all_gather(second_conv, "fsdp", axis=0, tiled=True)
    )
    top_hidden = (stacked_out.astype(jnp.float32) + gated(second_pre)).astype(jnp.bfloat16)
    incoming_gradient = cotangent[0].astype(jnp.float32)
    second_grad = gate_grad(second_pre, incoming_gradient).astype(jnp.bfloat16)
    second_shard = lax.psum_scatter(
        weight_term(closing_layer_input, second_grad).astype(jnp.bfloat16),
        "fsdp",
        scatter_dimension=0,
        tiled=True,
    )
    grad_second = lax.psum(second_shard, "tm").astype(jnp.float32)
    closing_backward = back_with(
        second_grad, lax.all_gather(second_conv, "fsdp", axis=0, tiled=True)
    )
    carried_back = passed_along(
        closing_backward[:, :channels].astype(jnp.bfloat16), "tm", -1
    ).astype(jnp.float32)
    opening_upstream_gradient = incoming_gradient + closing_backward[:, channels:] + carried_back
    first_grad = gate_grad(stacked_pre, opening_upstream_gradient).astype(jnp.bfloat16)
    first_shard = lax.psum_scatter(
        weight_term(opening_layer_input, first_grad).astype(jnp.bfloat16),
        "fsdp",
        scatter_dimension=0,
        tiled=True,
    )
    grad_first = lax.psum(first_shard, "tm").astype(jnp.float32)
    return (top_hidden[None], grad_first, grad_second)


def sigmoid(value):
    return 0.5 * jnp.tanh(0.5 * value) + 0.5


def kernel(
    frames, keep, w1_hbm, w2_hbm, cot,
    top, grad1, grad2,
    xs, ks, hs, x1, tail_in, out1, prev_out, w1, w2,
    th1, sg1, pre2, g, cb, cb_in,
    ends, part, core_in, core_sum, a_in, a_sum, b_in, b_sum, z_in, quarter,
    local_sem, gs, gr, es, er, ns, nr, os, orr, bs, br, ss, sr, zs, zr, qs, qr,
):
    T, F = 4, 8
    t, f = lax.axis_index("tm"), lax.axis_index("fsdp")
    x, c = t // 2, t % 2
    z, y = f // 2, f % 2
    place = c * 2 + x
    across = (1 - x) * 2 + c
    sibling = x * 2 + (1 - c)
    over_y = z * 2 + (1 - y)
    frames_n, ch = frames.shape
    seg = frames_n // SEGS
    lag = frames_n // 4
    shard = w1_hbm.shape[0]
    q = shard // T
    pending = []

    def rows(start, size):
        return pl.ds(pl.multiple_of(start, size), size)

    def send(src, dst, ssem, rsem, tm, fsdp):
        copy = pltpu.make_async_remote_copy(
            src_ref=src, dst_ref=dst, send_sem=ssem, recv_sem=rsem,
            device_id=(tm, fsdp), device_id_type=MESH,
        )
        copy.start()
        pending.append(copy)
        return copy

    own = [
        pltpu.make_async_copy(wh, w.at[rows(f * shard, shard), :], local_sem.at[m])
        for m, (wh, w) in enumerate(((w1_hbm, w1), (w2_hbm, w2)))
    ]
    for copy in own:
        copy.start()

    barrier = pltpu.get_barrier_semaphore()
    for k in range(1, F):
        pl.semaphore_signal(
            barrier, inc=1, device_id=(t, lax.rem(f + k, F)), device_id_type=MESH
        )
    for k in range(1, T):
        pl.semaphore_signal(
            barrier, inc=1, device_id=(lax.rem(t + k, T), f), device_id_type=MESH
        )
    pl.semaphore_wait(barrier, F + T - 2)

    half_rows = 2 * q
    Z = F // 2
    weights = (w1, w2)

    def quarter_of(w, owner, at):
        return w.at[rows(owner * shard + at * q, q), :]

    def half_of(w, owner):
        return w.at[rows(owner * shard + c * half_rows, half_rows), :]

    def hop(m, stage, k, src, dst, tm, fsdp):
        return send(src, dst, gs.at[m, stage, k], gr.at[m, stage, k], tm, fsdp)

    def zone(k):
        return lax.rem(z + Z - k, Z)

    def at_z(k):
        return lax.rem(z + k, Z) * 2 + y

    along = [
        [
            hop(m, 0, k, wh.at[rows(place * q, q), :], quarter_of(w, f, place), t, at_z(k))
            for k in range(1, Z)
        ]
        for m, (wh, w) in enumerate(((w1_hbm, w1), (w2_hbm, w2)))
    ]
    first_y = [
        hop(0, 2, 0, w1_hbm.at[rows(c * half_rows, half_rows), :], half_of(w1, f), t, over_y)
    ]
    second_y = [
        hop(1, 1, 0, w2_hbm.at[rows(place * q, q), :], quarter_of(w2, f, place), t, over_y)
    ]

    lanes = xs.shape[2]
    groups = ch // lanes

    @pl.loop(0, frames_n, step=64)
    def _(r):
        at = rows(r, 64)
        for j in range(groups):
            cols = pl.ds(j * lanes, lanes)
            xs[j, at, :] = frames[at, cols].astype(F32)
            ks[j, at, :] = keep[at, cols]

    def step(i, state):
        at = pl.ds(i, SEGS, stride=seg)
        new = []
        for j, (h, p) in enumerate(state):
            a = ks[j, at, :]
            h = a * h + (1.0 - a) * xs[j, at, :]
            p = p * a
            hs[j, at, :] = h
            ks[j, at, :] = p
            new.append((h, p))
        return tuple(new)

    nought = (jnp.zeros((SEGS, lanes), F32), jnp.ones((SEGS, lanes), F32))
    lax.fori_loop(0, seg, step, (nought,) * groups, unroll=4)
    before = []
    for j in range(groups):
        p, h = jnp.ones((1, lanes), F32), jnp.zeros((1, lanes), F32)
        before.append([])
        for s in range(SEGS):
            before[j].append((p, h))
            last = pl.ds((s + 1) * seg - 1, 1)
            p, h = ks[j, last, :] * p, ks[j, last, :] * h + hs[j, last, :]
        cols = pl.ds(j * lanes, lanes)
        ends[t, 0:8, cols] = jnp.broadcast_to(p, (8, lanes))
        ends[t, 8:16, cols] = jnp.broadcast_to(h, (8, lanes))
    states = [
        send(ends.at[t], ends.at[t], es.at[k], er.at[k], lax.rem(t + k, T), f)
        for k in range(1, T)
    ]
    first_x = []
    for k in range(1, Z):
        along[0][k - 1].wait_recv()
        mine = quarter_of(w1, zone(k) * 2 + y, place)
        first_x.append(hop(0, 1, k, mine, mine, across, f))
    for k in range(1, Z):
        along[1][k - 1].wait_recv()
        mine = quarter_of(w2, zone(k) * 2 + y, place)
        second_y.append(hop(1, 1, k, mine, mine, t, over_y))
    for copy in states:
        copy.wait_recv()
    carried = jnp.zeros((1, ch), F32)
    for j in range(T):
        pj = ends[j, 0:1, :]
        hj = ends[j, 8:9, :]
        carried = jnp.where(j < t, pj * carried + hj, carried)
    for j in range(groups):
        cols = slice(j * lanes, (j + 1) * lanes)
        for s in range(SEGS):
            pb, hb = before[j][s]
            start = hb + pb * carried[:, cols]
            at = pl.ds(s * seg, seg)
            x1[at, ch + j * lanes : ch + (j + 1) * lanes] = (
                xs[j, at, :] - (hs[j, at, :] + ks[j, at, :] * start)
            ).astype(BF16)

    def neighbour(src, dst, n, tm):
        return pltpu.make_async_remote_copy(
            src_ref=src, dst_ref=dst, send_sem=ns.at[n], recv_sem=nr.at[n],
            device_id=(tm, f), device_id_type=MESH,
        )

    nxt, prv = lax.rem(t + 1, T), lax.rem(t + T - 1, T)
    has_next, has_prev = t < T - 1, t > 0

    tail = neighbour(x1.at[pl.ds(frames_n - lag, lag), pl.ds(ch, ch)], tail_in, 0, nxt)
    pl.when(has_next)(tail.start)
    x1[lag:, :ch] = x1[: frames_n - lag, ch:]

    first_core, second_x, second_core = [], [], []
    for k in range(1, Z):
        first_x[k - 1].wait_recv()
        mine = half_of(w1, zone(k) * 2 + y)
        first_y.append(hop(0, 2, k, mine, mine, t, over_y))
        first_core.append(hop(0, 3, k, mine, mine, sibling, f))
    for k in range(1, Z):
        mine = quarter_of(w2, zone(k) * 2 + y, place)
        second_x.append(hop(1, 2, k, mine, mine, across, f))
    for k in range(Z):
        second_y[k].wait_recv()
        mine = quarter_of(w2, zone(k) * 2 + 1 - y, place)
        second_x.append(hop(1, 2, Z + k, mine, mine, across, f))
    for k in range(Z):
        first_y[k].wait_recv()
        mine = half_of(w1, zone(k) * 2 + 1 - y)
        first_core.append(hop(0, 3, Z + k, mine, mine, sibling, f))
    for copy in first_core:
        copy.wait_recv()
    own[0].wait()

    @pl.when(has_prev)
    def _():
        tail.wait_recv()
        x1[:lag, :ch] = tail_in[...]

    @pl.when(t == 0)
    def _():
        x1[:lag, :ch] = jnp.zeros((lag, ch), BF16)

    block = 128

    def blockwise(src, dst, ssems, rsems, tm):
        def copy(r):
            at = rows(r, block)
            return pltpu.make_async_remote_copy(
                src_ref=src.at[at, :], dst_ref=dst.at[at, :],
                send_sem=ssems.at[r // block], recv_sem=rsems.at[r // block],
                device_id=(tm, f), device_id_type=MESH,
            )

        return copy

    passed = blockwise(out1, prev_out, os, orr, nxt)
    back = blockwise(cb, cb_in, bs, br, prv)

    @pl.loop(0, frames_n, step=block)
    def _(r):
        at = rows(r, block)
        pre = jnp.dot(x1[at, :], w1[...], preferred_element_type=F32)
        th, sg = jnp.tanh(pre[:, :ch]), sigmoid(pre[:, ch:])
        th1[at, :] = th
        sg1[at, :] = sg
        out1[at, :] = (x1[at, ch:].astype(F32) + th * sg).astype(BF16)

        @pl.when(has_next)
        def _():
            passed(r).start()

    for k in range(2 * Z - 1):
        second_x[k].wait_recv()
        owner = zone(k + 1) * 2 + y if k < Z - 1 else zone(k - Z + 1) * 2 + 1 - y
        mine = half_of(w2, owner)
        second_core.append(hop(1, 3, k, mine, mine, sibling, f))

    @pl.when(t == 0)
    def _():
        prev_out[...] = jnp.zeros((frames_n, ch), BF16)

    for copy in second_core:
        copy.wait_recv()
    own[1].wait()

    @pl.loop(0, frames_n, step=block)
    def _(r):
        at = rows(r, block)

        @pl.when(has_prev)
        def _():
            passed(r).wait_recv()

        pre = jnp.dot(out1[at, :], w2[ch:, :], preferred_element_type=F32) + jnp.dot(
            prev_out[at, :], w2[:ch, :], preferred_element_type=F32
        )
        th, sg = jnp.tanh(pre[:, :ch]), sigmoid(pre[:, ch:])
        u = cot[at, :].astype(F32)
        top[at, :] = (out1[at, :].astype(F32) + th * sg).astype(BF16)
        g2 = jnp.concatenate(
            [u * sg * (1.0 - th * th), u * th * sg * (1.0 - sg)], axis=1
        ).astype(BF16)
        g[0, at, :] = g2
        cb[at, :] = lax.dot_general(
            g2, w2[:ch, :], (((1,), (1,)), ((), ())), preferred_element_type=F32
        ).astype(BF16)

        @pl.when(has_prev)
        def _():
            back(r).start()

    def partial(m, left, first_owner):
        @pl.loop(0, ch // shard)
        def _(j):
            cols = pl.ds(pl.multiple_of(j * shard, shard), shard)
            product = lax.dot_general(
                left[:, cols], g[m], (((0,), (0,)), ((), ())), preferred_element_type=F32
            )
            owner = first_owner + j
            part[m, owner // 2, owner % 2] = product.astype(BF16).reshape(2, 2, q, 2 * ch)

    two = Z // 2

    def span(h):
        return pl.ds(h * two, two)

    def core_phase(m, h):
        return send(part.at[m, span(h), :, 1 - c], core_in.at[m, span(h)],
                    ss.at[m, 0, h], sr.at[m, 0, h], sibling, f)

    def a_phase(m, h, copy):
        copy.wait_recv()
        for j in range(h * two, (h + 1) * two):
            for d in range(2):
                for e in range(2):
                    yy, xx = (d, e) if m == 0 else (e, d)
                    core_sum[m, d, j, e] = (
                        part[m, j, yy, c, xx].astype(F32) + core_in[m, j, yy, xx].astype(F32)
                    ).astype(BF16)
        mine, tm, fsdp = (y, t, over_y) if m == 0 else (x, across, f)
        return send(core_sum.at[m, 1 - mine, span(h)], a_in.at[m, span(h)],
                    ss.at[m, 1, h], sr.at[m, 1, h], tm, fsdp)

    def b_phase(m, h, copy):
        copy.wait_recv()
        mine = y if m == 0 else x
        for j in range(h * two, (h + 1) * two):
            for e in range(2):
                a_sum[m, e, j] = (
                    core_sum[m, mine, j, e].astype(F32) + a_in[m, j, e].astype(F32)
                ).astype(BF16)
        mine, tm, fsdp = (x, across, f) if m == 0 else (y, t, over_y)
        return send(a_sum.at[m, 1 - mine, span(h)], b_in.at[m, span(h)],
                    ss.at[m, 2, h], sr.at[m, 2, h], tm, fsdp)

    def z_copy(m, j, source):
        return pltpu.make_async_remote_copy(
            src_ref=b_sum.at[m, j], dst_ref=z_in.at[m, source],
            send_sem=zs.at[m, j], recv_sem=zr.at[m, source],
            device_id=(t, j * 2 + y), device_id_type=MESH,
        )

    def z_phase(m, h, copy):
        copy.wait_recv()
        mine = x if m == 0 else y
        for j in range(h * two, (h + 1) * two):
            b_sum[m, j] = (
                a_sum[m, mine, j].astype(F32) + b_in[m, j].astype(F32)
            ).astype(BF16)
            pl.when(z != j)(z_copy(m, j, z).start)

    def q_phase(m):
        total = b_sum[m, z].astype(F32)
        for k in range(1, Z):
            source = zone(k)
            z_copy(m, k, source).wait_recv()
            total += z_in[m, source].astype(F32)
        quarter[m, place] = total.astype(BF16)
        return [
            send(quarter.at[m, place], quarter.at[m, place], qs.at[m, k], qr.at[m, k],
                 lax.rem(t + k, T), f)
            for k in range(1, T)
        ]

    def finish(m, sends, grad):
        for copy in sends:
            copy.wait_recv()
        for j in range(T):
            grad[pl.ds(j * q, q), :] = quarter[m, j].astype(F32)

    half = ch // shard
    partial(0, prev_out, 0)
    core20 = core_phase(0, 0)
    partial(0, out1, half)
    core21 = core_phase(0, 1)
    a20 = a_phase(0, 0, core20)

    @pl.loop(0, frames_n, step=block)
    def _(r):
        at = rows(r, block)
        pre2[at, :] = cot[at, :].astype(F32) + lax.dot_general(
            g[0, at, :], w2[ch:, :], (((1,), (1,)), ((), ())), preferred_element_type=F32
        )

    a21 = a_phase(0, 1, core21)

    @pl.when(t == T - 1)
    def _():
        cb_in[...] = jnp.zeros((frames_n, ch), BF16)

    @pl.loop(0, frames_n, step=block)
    def _(r):
        at = rows(r, block)

        @pl.when(has_next)
        def _():
            back(r).wait_recv()

        u = pre2[at, :] + cb_in[at, :].astype(F32)
        th, sg = th1[at, :], sg1[at, :]
        g[1, at, :] = jnp.concatenate(
            [u * sg * (1.0 - th * th), u * th * sg * (1.0 - sg)], axis=1
        ).astype(BF16)

    partial(1, x1.at[:, pl.ds(0, ch)], 0)
    core10 = core_phase(1, 0)
    partial(1, x1.at[:, pl.ds(ch, ch)], half)
    core11 = core_phase(1, 1)
    a10 = a_phase(1, 0, core10)
    a11 = a_phase(1, 1, core11)
    b20 = b_phase(0, 0, a20)
    b21 = b_phase(0, 1, a21)
    b10 = b_phase(1, 0, a10)
    z_phase(0, 0, b20)
    z_phase(0, 1, b21)
    b11 = b_phase(1, 1, a11)
    z_phase(1, 0, b10)
    z_phase(1, 1, b11)
    last2 = q_phase(0)
    last1 = q_phase(1)
    finish(0, last2, grad2)
    finish(1, last1, grad1)

    for copy in pending:
        copy.wait_send()
    for m in range(2):
        for j in range(Z):
            pl.when(z != j)(z_copy(m, j, z).wait_send)
    pl.when(has_next)(tail.wait_send)
    for r in range(0, frames_n, block):
        pl.when(has_next)(passed(r).wait_send)
        pl.when(has_prev)(back(r).wait_send)


def fused(frames, retention, first_conv, second_conv, cotangent):
    _, n, ch = frames.shape
    shard, wide = first_conv.shape
    T, F, Z = 4, 8, 4
    q = shard // T
    vm = lambda shape, dtype: pltpu.VMEM(shape, dtype)
    dma = pltpu.SemaphoreType.DMA
    vspec = pl.BlockSpec(memory_space=pltpu.VMEM)
    anyspec = pl.BlockSpec(memory_space=pl.ANY)
    top, grad1, grad2 = pl.pallas_call(
        kernel,
        out_shape=(
            jax.ShapeDtypeStruct((n, ch), BF16),
            jax.ShapeDtypeStruct((shard, wide), F32),
            jax.ShapeDtypeStruct((shard, wide), F32),
        ),
        in_specs=[vspec, vspec, anyspec, anyspec, vspec],
        out_specs=(vspec, vspec, vspec),
        scratch_shapes=[
            vm((ch // 128, n, 128), F32), vm((ch // 128, n, 128), F32), vm((ch // 128, n, 128), F32),
            vm((n, wide), BF16), vm((n // 4, ch), BF16), vm((n, ch), BF16), vm((n, ch), BF16),
            vm((wide, wide), BF16), vm((wide, wide), BF16),
            vm((n, ch), F32), vm((n, ch), F32), vm((n, ch), F32),
            vm((2, n, wide), BF16), vm((n, ch), BF16), vm((n, ch), BF16),
            vm((T, 16, ch), F32),
            vm((2, Z, 2, 2, 2, q, wide), BF16), vm((2, Z, 2, 2, q, wide), BF16),
            vm((2, 2, Z, 2, q, wide), BF16), vm((2, Z, 2, q, wide), BF16),
            vm((2, 2, Z, q, wide), BF16), vm((2, Z, q, wide), BF16),
            vm((2, Z, q, wide), BF16), vm((2, Z, q, wide), BF16),
            vm((2, T, q, wide), BF16),
            dma((2,)), dma((2, 4, F)), dma((2, 4, F)), dma((T,)), dma((T,)),
            dma((1,)), dma((1,)), dma((4,)), dma((4,)), dma((4,)), dma((4,)),
            dma((2, 3, 2)), dma((2, 3, 2)), dma((2, Z)), dma((2, Z)),
            dma((2, T)), dma((2, T)),
        ],
        compiler_params=pltpu.CompilerParams(
            collective_id=0, has_side_effects=True, vmem_limit_bytes=56 * 2**20
        ),
        cost_estimate=pl.CostEstimate(
            flops=10 * n * wide * wide, bytes_accessed=8 * n * wide, transcendentals=2 * n * wide
        ),
    )(frames[0], retention[0], first_conv, second_conv, cotangent[0])
    return (top[None], grad1, grad2)


def solution(mesh):
    fits = mesh.shape["tm"] == 4 and mesh.shape["fsdp"] == 8
    in_specs = (
        P("fsdp", "tm", None),
        P("fsdp", "tm", None),
        P("fsdp", None),
        P("fsdp", None),
        P("fsdp", "tm", None),
    )
    out_specs = (P("fsdp", "tm", None), P("fsdp", None), P("fsdp", None))
    return jax.shard_map(
        fused if fits else on_device,
        mesh=mesh,
        in_specs=in_specs,
        out_specs=out_specs,
        check_vma=False,
    )
```

```python
import jax
import jax.numpy as jnp
from jax import lax
from jax.experimental import pallas as pl
from jax.experimental.pallas import tpu as pltpu
from jax.sharding import PartitionSpec as P

MESH = pl.DeviceIdType.MESH
F32 = jnp.float32
BF16 = jnp.bfloat16
SEGS = 8


def prefix(part, axis, combine, identity):
    place = lax.axis_index(axis)
    gathered = jax.tree.map(lambda a: lax.all_gather(a, axis), part)
    state = jax.tree.map(lambda a, e: jnp.zeros_like(a) + jnp.asarray(e, a.dtype), part, identity)

    def one(step, state):
        return combine(
            state, jax.tree.map(lambda a: lax.dynamic_index_in_dim(a, step, 0, False), gathered)
        )

    return lax.fori_loop(0, place, one, state)


def passed_along(value, axis, steps):
    count = lax.axis_size(axis)
    leading, last = (max(0, -steps), min(count, count - steps))
    return lax.ppermute(value, axis, [(source, source + steps) for source in range(leading, last)])


def combine_maps(earlier, later):
    return (earlier[0] * later[0], later[0] * earlier[1] + later[1])


def gated(pre_values):
    split_at = pre_values.shape[1] // 2
    return jnp.tanh(pre_values[:, :split_at]) * jax.nn.sigmoid(pre_values[:, split_at:])


def gate_grad(pre_values, incoming_gradient):
    split_at = pre_values.shape[1] // 2
    tanh_part = jnp.tanh(pre_values[:, :split_at])
    gate_part = jax.nn.sigmoid(pre_values[:, split_at:])
    return jnp.concatenate(
        [
            incoming_gradient * gate_part * (1.0 - tanh_part * tanh_part),
            incoming_gradient * tanh_part * gate_part * (1.0 - gate_part),
        ],
        axis=1,
    )


def accumulate_with(operand, weights_block):
    return jnp.dot(operand, weights_block, preferred_element_type=jnp.float32)


def back_with(gradients, weights_block):
    return lax.dot_general(
        gradients, weights_block, (((1,), (1,)), ((), ())), preferred_element_type=jnp.float32
    )


def weight_term(operand, gradients):
    return lax.dot_general(
        operand, gradients, (((0,), (0,)), ((), ())), preferred_element_type=jnp.float32
    )


def on_device(frames, retention, first_conv, second_conv, cotangent):
    payload_elements = frames[0].astype(jnp.float32)
    keep_rate = retention[0]
    length, channels = payload_elements.shape
    short_lag = length // 4
    factor, local_part = lax.associative_scan(
        combine_maps, (keep_rate, (1.0 - keep_rate) * payload_elements), axis=0
    )
    identity_map = (jnp.ones((channels,), jnp.float32), jnp.zeros((channels,), jnp.float32))
    carried_in = prefix((factor[-1], local_part[-1]), "tm", combine_maps, identity_map)
    trend_removed = (payload_elements - (local_part + factor * carried_in[1][None, :])).astype(
        jnp.bfloat16
    )
    tail_rows = trend_removed[length - short_lag :]
    near_tail = passed_along(tail_rows, "tm", 1)
    own_past = jnp.concatenate([near_tail, trend_removed[: length - short_lag]], axis=0)
    opening_layer_input = jnp.concatenate([own_past, trend_removed], axis=1)
    stacked_pre = accumulate_with(
        opening_layer_input, lax.all_gather(first_conv, "fsdp", axis=0, tiled=True)
    )
    stacked_out = (trend_removed.astype(jnp.float32) + gated(stacked_pre)).astype(jnp.bfloat16)
    earlier_out = passed_along(stacked_out, "tm", 1)
    closing_layer_input = jnp.concatenate([earlier_out, stacked_out], axis=1)
    second_pre = accumulate_with(
        closing_layer_input, lax.all_gather(second_conv, "fsdp", axis=0, tiled=True)
    )
    top_hidden = (stacked_out.astype(jnp.float32) + gated(second_pre)).astype(jnp.bfloat16)
    incoming_gradient = cotangent[0].astype(jnp.float32)
    second_grad = gate_grad(second_pre, incoming_gradient).astype(jnp.bfloat16)
    second_shard = lax.psum_scatter(
        weight_term(closing_layer_input, second_grad).astype(jnp.bfloat16),
        "fsdp",
        scatter_dimension=0,
        tiled=True,
    )
    grad_second = lax.psum(second_shard, "tm").astype(jnp.float32)
    closing_backward = back_with(
        second_grad, lax.all_gather(second_conv, "fsdp", axis=0, tiled=True)
    )
    carried_back = passed_along(
        closing_backward[:, :channels].astype(jnp.bfloat16), "tm", -1
    ).astype(jnp.float32)
    opening_upstream_gradient = incoming_gradient + closing_backward[:, channels:] + carried_back
    first_grad = gate_grad(stacked_pre, opening_upstream_gradient).astype(jnp.bfloat16)
    first_shard = lax.psum_scatter(
        weight_term(opening_layer_input, first_grad).astype(jnp.bfloat16),
        "fsdp",
        scatter_dimension=0,
        tiled=True,
    )
    grad_first = lax.psum(first_shard, "tm").astype(jnp.float32)
    return (top_hidden[None], grad_first, grad_second)


def sigmoid(value):
    return 0.5 * jnp.tanh(0.5 * value) + 0.5


def kernel(
    frames, keep, w1_hbm, w2_hbm, cot,
    top, grad1, grad2,
    xs, ks, hs, x1, tail_in, out1, prev_out, w1, w2,
    th1, sg1, pre2, g, cb, cb_in,
    ends, part, core_in, core_sum, a_in, a_sum, b_in, b_sum, z_in, quarter,
    local_sem, gs, gr, es, er, ns, nr, os, orr, bs, br, ss, sr, zs, zr, qs, qr,
):
    T, F = 4, 8
    t, f = lax.axis_index("tm"), lax.axis_index("fsdp")
    x, c = t // 2, t % 2
    z, y = f // 2, f % 2
    place = c * 2 + x
    across = (1 - x) * 2 + c
    sibling = x * 2 + (1 - c)
    over_y = z * 2 + (1 - y)
    frames_n, ch = frames.shape
    seg = frames_n // SEGS
    lag = frames_n // 4
    shard = w1_hbm.shape[0]
    q = shard // T
    pending = []

    def rows(start, size):
        return pl.ds(pl.multiple_of(start, size), size)

    def send(src, dst, ssem, rsem, tm, fsdp):
        copy = pltpu.make_async_remote_copy(
            src_ref=src, dst_ref=dst, send_sem=ssem, recv_sem=rsem,
            device_id=(tm, fsdp), device_id_type=MESH,
        )
        copy.start()
        pending.append(copy)
        return copy

    own = [
        pltpu.make_async_copy(wh, w.at[rows(f * shard, shard), :], local_sem.at[m])
        for m, (wh, w) in enumerate(((w1_hbm, w1), (w2_hbm, w2)))
    ]
    for copy in own:
        copy.start()

    barrier = pltpu.get_barrier_semaphore()
    for k in range(1, F):
        pl.semaphore_signal(
            barrier, inc=1, device_id=(t, lax.rem(f + k, F)), device_id_type=MESH
        )
    for k in range(1, T):
        pl.semaphore_signal(
            barrier, inc=1, device_id=(lax.rem(t + k, T), f), device_id_type=MESH
        )
    pl.semaphore_wait(barrier, F + T - 2)

    half_rows = 2 * q
    Z = F // 2
    weights = (w1, w2)

    def quarter_of(w, owner, at):
        return w.at[rows(owner * shard + at * q, q), :]

    def half_of(w, owner):
        return w.at[rows(owner * shard + c * half_rows, half_rows), :]

    def hop(m, stage, k, src, dst, tm, fsdp):
        return send(src, dst, gs.at[m, stage, k], gr.at[m, stage, k], tm, fsdp)

    def zone(k):
        return lax.rem(z + Z - k, Z)

    def at_z(k):
        return lax.rem(z + k, Z) * 2 + y

    shards = (w1_hbm, w2_hbm)

    def start_z(m):
        return [
            hop(m, 0, k, shards[m].at[rows(place * q, q), :],
                quarter_of(weights[m], f, place), t, at_z(k))
            for k in range(1, Z)
        ]

    def start_y(m):
        return [
            hop(m, 2, 0, shards[m].at[rows(c * half_rows, half_rows), :],
                half_of(weights[m], f), t, over_y)
        ]

    def spread_xy(m, came_z, went_y):
        went_x = []
        for k in range(1, Z):
            came_z[k - 1].wait_recv()
            mine = quarter_of(weights[m], zone(k) * 2 + y, place)
            went_x.append(hop(m, 1, k, mine, mine, across, f))
            went_y.append(hop(m, 2, k, mine, mine, t, over_y))
        return went_x

    def spread_diagonal(m, went_y):
        went = []
        went_y[0].wait_recv()
        for k in range(1, Z):
            went_y[k].wait_recv()
            mine = quarter_of(weights[m], zone(k) * 2 + 1 - y, place)
            went.append(hop(m, 1, Z + k, mine, mine, across, f))
        return went

    def spread_core(m, went_x, diagonal):
        went = []
        for k in range(Z):
            if k:
                went_x[k - 1].wait_recv()
                mine = half_of(weights[m], zone(k) * 2 + y)
                went.append(hop(m, 3, k, mine, mine, sibling, f))
                diagonal[k - 1].wait_recv()
            mine = half_of(weights[m], zone(k) * 2 + 1 - y)
            went.append(hop(m, 3, Z + k, mine, mine, sibling, f))
        for copy in went:
            copy.wait_recv()
        own[m].wait()

    first_z = start_z(0)
    first_y = start_y(0)

    lanes = xs.shape[2]
    groups = ch // lanes

    @pl.loop(0, frames_n, step=64)
    def _(r):
        at = rows(r, 64)
        for j in range(groups):
            cols = pl.ds(j * lanes, lanes)
            xs[j, at, :] = frames[at, cols].astype(F32)
            ks[j, at, :] = keep[at, cols]

    def step(i, state):
        at = pl.ds(i, SEGS, stride=seg)
        new = []
        for j, (h, p) in enumerate(state):
            a = ks[j, at, :]
            h = a * h + (1.0 - a) * xs[j, at, :]
            p = p * a
            hs[j, at, :] = h
            ks[j, at, :] = p
            new.append((h, p))
        return tuple(new)

    nought = (jnp.zeros((SEGS, lanes), F32), jnp.ones((SEGS, lanes), F32))
    lax.fori_loop(0, seg, step, (nought,) * groups, unroll=4)
    before = []
    for j in range(groups):
        p, h = jnp.ones((1, lanes), F32), jnp.zeros((1, lanes), F32)
        before.append([])
        for s in range(SEGS):
            before[j].append((p, h))
            last = pl.ds((s + 1) * seg - 1, 1)
            p, h = ks[j, last, :] * p, ks[j, last, :] * h + hs[j, last, :]
        cols = pl.ds(j * lanes, lanes)
        ends[t, 0:8, cols] = jnp.broadcast_to(p, (8, lanes))
        ends[t, 8:16, cols] = jnp.broadcast_to(h, (8, lanes))
    states = [
        send(ends.at[t], ends.at[t], es.at[k], er.at[k], lax.rem(t + k, T), f)
        for k in range(1, T)
    ]
    first_x = spread_xy(0, first_z, first_y)
    second_z = start_z(1)
    second_y = start_y(1)
    for copy in states:
        copy.wait_recv()
    carried = jnp.zeros((1, ch), F32)
    for j in range(T):
        pj = ends[j, 0:1, :]
        hj = ends[j, 8:9, :]
        carried = jnp.where(j < t, pj * carried + hj, carried)
    for j in range(groups):
        cols = slice(j * lanes, (j + 1) * lanes)
        for s in range(SEGS):
            pb, hb = before[j][s]
            start = hb + pb * carried[:, cols]
            at = pl.ds(s * seg, seg)
            x1[at, ch + j * lanes : ch + (j + 1) * lanes] = (
                xs[j, at, :] - (hs[j, at, :] + ks[j, at, :] * start)
            ).astype(BF16)

    def neighbour(src, dst, n, tm):
        return pltpu.make_async_remote_copy(
            src_ref=src, dst_ref=dst, send_sem=ns.at[n], recv_sem=nr.at[n],
            device_id=(tm, f), device_id_type=MESH,
        )

    nxt, prv = lax.rem(t + 1, T), lax.rem(t + T - 1, T)
    has_next, has_prev = t < T - 1, t > 0

    tail = neighbour(x1.at[pl.ds(frames_n - lag, lag), pl.ds(ch, ch)], tail_in, 0, nxt)
    pl.when(has_next)(tail.start)
    x1[lag:, :ch] = x1[: frames_n - lag, ch:]

    first_diagonal = spread_diagonal(0, first_y)
    second_x = spread_xy(1, second_z, second_y)
    spread_core(0, first_x, first_diagonal)

    @pl.when(has_prev)
    def _():
        tail.wait_recv()
        x1[:lag, :ch] = tail_in[...]

    @pl.when(t == 0)
    def _():
        x1[:lag, :ch] = jnp.zeros((lag, ch), BF16)

    block = 128

    def blockwise(src, dst, ssems, rsems, tm):
        def copy(r):
            at = rows(r, block)
            return pltpu.make_async_remote_copy(
                src_ref=src.at[at, :], dst_ref=dst.at[at, :],
                send_sem=ssems.at[r // block], recv_sem=rsems.at[r // block],
                device_id=(tm, f), device_id_type=MESH,
            )

        return copy

    passed = blockwise(out1, prev_out, os, orr, nxt)
    back = blockwise(cb, cb_in, bs, br, prv)

    @pl.loop(0, frames_n, step=block)
    def _(r):
        at = rows(r, block)
        pre = jnp.dot(x1[at, :], w1[...], preferred_element_type=F32)
        th, sg = jnp.tanh(pre[:, :ch]), sigmoid(pre[:, ch:])
        th1[at, :] = th
        sg1[at, :] = sg
        out1[at, :] = (x1[at, ch:].astype(F32) + th * sg).astype(BF16)

        @pl.when(has_next)
        def _():
            passed(r).start()

    second_diagonal = spread_diagonal(1, second_y)

    @pl.when(t == 0)
    def _():
        prev_out[...] = jnp.zeros((frames_n, ch), BF16)

    spread_core(1, second_x, second_diagonal)

    @pl.loop(0, frames_n, step=block)
    def _(r):
        at = rows(r, block)

        @pl.when(has_prev)
        def _():
            passed(r).wait_recv()

        pre = jnp.dot(out1[at, :], w2[ch:, :], preferred_element_type=F32) + jnp.dot(
            prev_out[at, :], w2[:ch, :], preferred_element_type=F32
        )
        th, sg = jnp.tanh(pre[:, :ch]), sigmoid(pre[:, ch:])
        u = cot[at, :].astype(F32)
        top[at, :] = (out1[at, :].astype(F32) + th * sg).astype(BF16)
        g2 = jnp.concatenate(
            [u * sg * (1.0 - th * th), u * th * sg * (1.0 - sg)], axis=1
        ).astype(BF16)
        g[0, at, :] = g2
        cb[at, :] = lax.dot_general(
            g2, w2[:ch, :], (((1,), (1,)), ((), ())), preferred_element_type=F32
        ).astype(BF16)

        @pl.when(has_prev)
        def _():
            back(r).start()

    def partial(m, left, first_owner):
        @pl.loop(0, ch // shard)
        def _(j):
            cols = pl.ds(pl.multiple_of(j * shard, shard), shard)
            product = lax.dot_general(
                left[:, cols], g[m], (((0,), (0,)), ((), ())), preferred_element_type=F32
            )
            owner = first_owner + j
            part[m, owner // 2, owner % 2] = product.astype(BF16).reshape(2, 2, q, 2 * ch)

    two = Z // 2

    def span(h):
        return pl.ds(h * two, two)

    def core_phase(m, h):
        return send(part.at[m, span(h), :, 1 - c], core_in.at[m, span(h)],
                    ss.at[m, 0, h], sr.at[m, 0, h], sibling, f)

    def a_phase(m, h, copy):
        copy.wait_recv()
        for j in range(h * two, (h + 1) * two):
            for d in range(2):
                for e in range(2):
                    yy, xx = (d, e) if h == 0 else (e, d)
                    core_sum[m, d, j, e] = (
                        part[m, j, yy, c, xx].astype(F32) + core_in[m, j, yy, xx].astype(F32)
                    ).astype(BF16)
        mine, tm, fsdp = (y, t, over_y) if h == 0 else (x, across, f)
        return send(core_sum.at[m, 1 - mine, span(h)], a_in.at[m, span(h)],
                    ss.at[m, 1, h], sr.at[m, 1, h], tm, fsdp)

    def b_phase(m, h, copy):
        copy.wait_recv()
        mine = y if h == 0 else x
        for j in range(h * two, (h + 1) * two):
            for e in range(2):
                a_sum[m, e, j] = (
                    core_sum[m, mine, j, e].astype(F32) + a_in[m, j, e].astype(F32)
                ).astype(BF16)
        mine, tm, fsdp = (x, across, f) if h == 0 else (y, t, over_y)
        return send(a_sum.at[m, 1 - mine, span(h)], b_in.at[m, span(h)],
                    ss.at[m, 2, h], sr.at[m, 2, h], tm, fsdp)

    def z_copy(m, j, source):
        return pltpu.make_async_remote_copy(
            src_ref=b_sum.at[m, j], dst_ref=z_in.at[m, source],
            send_sem=zs.at[m, j], recv_sem=zr.at[m, source],
            device_id=(t, j * 2 + y), device_id_type=MESH,
        )

    def z_phase(m, h, copy):
        copy.wait_recv()
        mine = x if h == 0 else y
        for j in range(h * two, (h + 1) * two):
            b_sum[m, j] = (
                a_sum[m, mine, j].astype(F32) + b_in[m, j].astype(F32)
            ).astype(BF16)
            pl.when(z != j)(z_copy(m, j, z).start)

    def q_phase(m):
        total = b_sum[m, z].astype(F32)
        for k in range(1, Z):
            source = zone(k)
            z_copy(m, k, source).wait_recv()
            total += z_in[m, source].astype(F32)
        quarter[m, place] = total.astype(BF16)
        return [
            send(quarter.at[m, place], quarter.at[m, place], qs.at[m, k], qr.at[m, k],
                 lax.rem(t + k, T), f)
            for k in range(1, T)
        ]

    def finish(m, sends, grad):
        for copy in sends:
            copy.wait_recv()
        for j in range(T):
            grad[pl.ds(j * q, q), :] = quarter[m, j].astype(F32)

    half = ch // shard
    partial(0, prev_out, 0)
    core20 = core_phase(0, 0)
    partial(0, out1, half)
    core21 = core_phase(0, 1)
    a20 = a_phase(0, 0, core20)

    @pl.loop(0, frames_n, step=block)
    def _(r):
        at = rows(r, block)
        pre2[at, :] = cot[at, :].astype(F32) + lax.dot_general(
            g[0, at, :], w2[ch:, :], (((1,), (1,)), ((), ())), preferred_element_type=F32
        )

    a21 = a_phase(0, 1, core21)

    @pl.when(t == T - 1)
    def _():
        cb_in[...] = jnp.zeros((frames_n, ch), BF16)

    @pl.loop(0, frames_n, step=block)
    def _(r):
        at = rows(r, block)

        @pl.when(has_next)
        def _():
            back(r).wait_recv()

        u = pre2[at, :] + cb_in[at, :].astype(F32)
        th, sg = th1[at, :], sg1[at, :]
        g[1, at, :] = jnp.concatenate(
            [u * sg * (1.0 - th * th), u * th * sg * (1.0 - sg)], axis=1
        ).astype(BF16)

    partial(1, x1.at[:, pl.ds(0, ch)], 0)
    core10 = core_phase(1, 0)
    partial(1, x1.at[:, pl.ds(ch, ch)], half)
    core11 = core_phase(1, 1)
    a10 = a_phase(1, 0, core10)
    a11 = a_phase(1, 1, core11)
    b20 = b_phase(0, 0, a20)
    b21 = b_phase(0, 1, a21)
    b10 = b_phase(1, 0, a10)
    b11 = b_phase(1, 1, a11)
    z_phase(0, 0, b20)
    z_phase(0, 1, b21)
    z_phase(1, 0, b10)
    z_phase(1, 1, b11)
    last2 = q_phase(0)
    last1 = q_phase(1)
    finish(0, last2, grad2)
    finish(1, last1, grad1)

    for copy in pending:
        copy.wait_send()
    for m in range(2):
        for j in range(Z):
            pl.when(z != j)(z_copy(m, j, z).wait_send)
    pl.when(has_next)(tail.wait_send)
    for r in range(0, frames_n, block):
        pl.when(has_next)(passed(r).wait_send)
        pl.when(has_prev)(back(r).wait_send)


def fused(frames, retention, first_conv, second_conv, cotangent):
    _, n, ch = frames.shape
    shard, wide = first_conv.shape
    T, F, Z = 4, 8, 4
    q = shard // T
    vm = lambda shape, dtype: pltpu.VMEM(shape, dtype)
    dma = pltpu.SemaphoreType.DMA
    vspec = pl.BlockSpec(memory_space=pltpu.VMEM)
    anyspec = pl.BlockSpec(memory_space=pl.ANY)
    top, grad1, grad2 = pl.pallas_call(
        kernel,
        out_shape=(
            jax.ShapeDtypeStruct((n, ch), BF16),
            jax.ShapeDtypeStruct((shard, wide), F32),
            jax.ShapeDtypeStruct((shard, wide), F32),
        ),
        in_specs=[vspec, vspec, anyspec, anyspec, vspec],
        out_specs=(vspec, vspec, vspec),
        scratch_shapes=[
            vm((ch // 128, n, 128), F32), vm((ch // 128, n, 128), F32), vm((ch // 128, n, 128), F32),
            vm((n, wide), BF16), vm((n // 4, ch), BF16), vm((n, ch), BF16), vm((n, ch), BF16),
            vm((wide, wide), BF16), vm((wide, wide), BF16),
            vm((n, ch), F32), vm((n, ch), F32), vm((n, ch), F32),
            vm((2, n, wide), BF16), vm((n, ch), BF16), vm((n, ch), BF16),
            vm((T, 16, ch), F32),
            vm((2, Z, 2, 2, 2, q, wide), BF16), vm((2, Z, 2, 2, q, wide), BF16),
            vm((2, 2, Z, 2, q, wide), BF16), vm((2, Z, 2, q, wide), BF16),
            vm((2, 2, Z, q, wide), BF16), vm((2, Z, q, wide), BF16),
            vm((2, Z, q, wide), BF16), vm((2, Z, q, wide), BF16),
            vm((2, T, q, wide), BF16),
            dma((2,)), dma((2, 4, F)), dma((2, 4, F)), dma((T,)), dma((T,)),
            dma((1,)), dma((1,)), dma((4,)), dma((4,)), dma((4,)), dma((4,)),
            dma((2, 3, 2)), dma((2, 3, 2)), dma((2, Z)), dma((2, Z)),
            dma((2, T)), dma((2, T)),
        ],
        compiler_params=pltpu.CompilerParams(
            collective_id=0, has_side_effects=True, vmem_limit_bytes=56 * 2**20
        ),
        cost_estimate=pl.CostEstimate(
            flops=10 * n * wide * wide, bytes_accessed=8 * n * wide, transcendentals=2 * n * wide
        ),
    )(frames[0], retention[0], first_conv, second_conv, cotangent[0])
    return (top[None], grad1, grad2)


def solution(mesh):
    fits = mesh.shape["tm"] == 4 and mesh.shape["fsdp"] == 8
    in_specs = (
        P("fsdp", "tm", None),
        P("fsdp", "tm", None),
        P("fsdp", None),
        P("fsdp", None),
        P("fsdp", "tm", None),
    )
    out_specs = (P("fsdp", "tm", None), P("fsdp", None), P("fsdp", None))
    return jax.shard_map(
        fused if fits else on_device,
        mesh=mesh,
        in_specs=in_specs,
        out_specs=out_specs,
        check_vma=False,
    )
```

```python
import jax
import jax.numpy as jnp
from jax import lax
from jax.experimental import pallas as pl
from jax.experimental.pallas import tpu as pltpu
from jax.sharding import PartitionSpec as P

MESH = pl.DeviceIdType.MESH
F32 = jnp.float32
BF16 = jnp.bfloat16
SEGS = 8


def prefix(part, axis, combine, identity):
    place = lax.axis_index(axis)
    gathered = jax.tree.map(lambda a: lax.all_gather(a, axis), part)
    state = jax.tree.map(lambda a, e: jnp.zeros_like(a) + jnp.asarray(e, a.dtype), part, identity)

    def one(step, state):
        return combine(
            state, jax.tree.map(lambda a: lax.dynamic_index_in_dim(a, step, 0, False), gathered)
        )

    return lax.fori_loop(0, place, one, state)


def passed_along(value, axis, steps):
    count = lax.axis_size(axis)
    leading, last = (max(0, -steps), min(count, count - steps))
    return lax.ppermute(value, axis, [(source, source + steps) for source in range(leading, last)])


def combine_maps(earlier, later):
    return (earlier[0] * later[0], later[0] * earlier[1] + later[1])


def gated(pre_values):
    split_at = pre_values.shape[1] // 2
    return jnp.tanh(pre_values[:, :split_at]) * jax.nn.sigmoid(pre_values[:, split_at:])


def gate_grad(pre_values, incoming_gradient):
    split_at = pre_values.shape[1] // 2
    tanh_part = jnp.tanh(pre_values[:, :split_at])
    gate_part = jax.nn.sigmoid(pre_values[:, split_at:])
    return jnp.concatenate(
        [
            incoming_gradient * gate_part * (1.0 - tanh_part * tanh_part),
            incoming_gradient * tanh_part * gate_part * (1.0 - gate_part),
        ],
        axis=1,
    )


def accumulate_with(operand, weights_block):
    return jnp.dot(operand, weights_block, preferred_element_type=jnp.float32)


def back_with(gradients, weights_block):
    return lax.dot_general(
        gradients, weights_block, (((1,), (1,)), ((), ())), preferred_element_type=jnp.float32
    )


def weight_term(operand, gradients):
    return lax.dot_general(
        operand, gradients, (((0,), (0,)), ((), ())), preferred_element_type=jnp.float32
    )


def on_device(frames, retention, first_conv, second_conv, cotangent):
    payload_elements = frames[0].astype(jnp.float32)
    keep_rate = retention[0]
    length, channels = payload_elements.shape
    short_lag = length // 4
    factor, local_part = lax.associative_scan(
        combine_maps, (keep_rate, (1.0 - keep_rate) * payload_elements), axis=0
    )
    identity_map = (jnp.ones((channels,), jnp.float32), jnp.zeros((channels,), jnp.float32))
    carried_in = prefix((factor[-1], local_part[-1]), "tm", combine_maps, identity_map)
    trend_removed = (payload_elements - (local_part + factor * carried_in[1][None, :])).astype(
        jnp.bfloat16
    )
    tail_rows = trend_removed[length - short_lag :]
    near_tail = passed_along(tail_rows, "tm", 1)
    own_past = jnp.concatenate([near_tail, trend_removed[: length - short_lag]], axis=0)
    opening_layer_input = jnp.concatenate([own_past, trend_removed], axis=1)
    stacked_pre = accumulate_with(
        opening_layer_input, lax.all_gather(first_conv, "fsdp", axis=0, tiled=True)
    )
    stacked_out = (trend_removed.astype(jnp.float32) + gated(stacked_pre)).astype(jnp.bfloat16)
    earlier_out = passed_along(stacked_out, "tm", 1)
    closing_layer_input = jnp.concatenate([earlier_out, stacked_out], axis=1)
    second_pre = accumulate_with(
        closing_layer_input, lax.all_gather(second_conv, "fsdp", axis=0, tiled=True)
    )
    top_hidden = (stacked_out.astype(jnp.float32) + gated(second_pre)).astype(jnp.bfloat16)
    incoming_gradient = cotangent[0].astype(jnp.float32)
    second_grad = gate_grad(second_pre, incoming_gradient).astype(jnp.bfloat16)
    second_shard = lax.psum_scatter(
        weight_term(closing_layer_input, second_grad).astype(jnp.bfloat16),
        "fsdp",
        scatter_dimension=0,
        tiled=True,
    )
    grad_second = lax.psum(second_shard, "tm").astype(jnp.float32)
    closing_backward = back_with(
        second_grad, lax.all_gather(second_conv, "fsdp", axis=0, tiled=True)
    )
    carried_back = passed_along(
        closing_backward[:, :channels].astype(jnp.bfloat16), "tm", -1
    ).astype(jnp.float32)
    opening_upstream_gradient = incoming_gradient + closing_backward[:, channels:] + carried_back
    first_grad = gate_grad(stacked_pre, opening_upstream_gradient).astype(jnp.bfloat16)
    first_shard = lax.psum_scatter(
        weight_term(opening_layer_input, first_grad).astype(jnp.bfloat16),
        "fsdp",
        scatter_dimension=0,
        tiled=True,
    )
    grad_first = lax.psum(first_shard, "tm").astype(jnp.float32)
    return (top_hidden[None], grad_first, grad_second)


def sigmoid(value):
    return 0.5 * jnp.tanh(0.5 * value) + 0.5


def kernel(
    frames, keep, w1_hbm, w2_hbm, cot,
    top, grad1, grad2,
    xs, ks, hs, x1, tail_in, out1, prev_out, w1, w2,
    th1, sg1, pre2, g, cb, cb_in,
    ends, part, core_in, core_sum, a_in, a_sum, b_in, b_sum, z_in, quarter,
    local_sem, gs, gr, es, er, ns, nr, os, orr, bs, br, ss, sr, zs, zr, qs, qr,
):
    T, F = 4, 8
    t, f = lax.axis_index("tm"), lax.axis_index("fsdp")
    x, c = t // 2, t % 2
    z, y = f // 2, f % 2
    place = c * 2 + x
    across = (1 - x) * 2 + c
    sibling = x * 2 + (1 - c)
    over_y = z * 2 + (1 - y)
    frames_n, ch = frames.shape
    seg = frames_n // SEGS
    lag = frames_n // 4
    shard = w1_hbm.shape[0]
    q = shard // T
    pending = []

    def rows(start, size):
        return pl.ds(pl.multiple_of(start, size), size)

    def send(src, dst, ssem, rsem, tm, fsdp):
        copy = pltpu.make_async_remote_copy(
            src_ref=src, dst_ref=dst, send_sem=ssem, recv_sem=rsem,
            device_id=(tm, fsdp), device_id_type=MESH,
        )
        copy.start()
        pending.append(copy)
        return copy

    own = [
        pltpu.make_async_copy(wh, w.at[rows(f * shard, shard), :], local_sem.at[m])
        for m, (wh, w) in enumerate(((w1_hbm, w1), (w2_hbm, w2)))
    ]
    for copy in own:
        copy.start()

    barrier = pltpu.get_barrier_semaphore()
    for k in range(1, F):
        pl.semaphore_signal(
            barrier, inc=1, device_id=(t, lax.rem(f + k, F)), device_id_type=MESH
        )
    for k in range(1, T):
        pl.semaphore_signal(
            barrier, inc=1, device_id=(lax.rem(t + k, T), f), device_id_type=MESH
        )
    pl.semaphore_wait(barrier, F + T - 2)

    half_rows = 2 * q
    Z = F // 2
    weights = (w1, w2)

    def quarter_of(w, owner, at):
        return w.at[rows(owner * shard + at * q, q), :]

    def half_of(w, owner):
        return w.at[rows(owner * shard + c * half_rows, half_rows), :]

    def hop(m, stage, k, src, dst, tm, fsdp):
        return send(src, dst, gs.at[m, stage, k], gr.at[m, stage, k], tm, fsdp)

    def zone(k):
        return lax.rem(z + Z - k, Z)

    def at_z(k):
        return lax.rem(z + k, Z) * 2 + y

    shards = (w1_hbm, w2_hbm)

    def start_z(m):
        return [
            hop(m, 0, k, shards[m].at[rows(place * q, q), :],
                quarter_of(weights[m], f, place), t, at_z(k))
            for k in range(1, Z)
        ]

    def start_y(m):
        return [
            hop(m, 2, 0, shards[m].at[rows(c * half_rows, half_rows), :],
                half_of(weights[m], f), t, over_y)
        ]

    def spread_xy(m, came_z, went_y):
        went_x = []
        for k in range(1, Z):
            came_z[k - 1].wait_recv()
            mine = quarter_of(weights[m], zone(k) * 2 + y, place)
            went_x.append(hop(m, 1, k, mine, mine, across, f))
            went_y.append(hop(m, 2, k, mine, mine, t, over_y))
        return went_x

    def spread_diagonal(m, went_y):
        went = []
        went_y[0].wait_recv()
        for k in range(1, Z):
            went_y[k].wait_recv()
            mine = quarter_of(weights[m], zone(k) * 2 + 1 - y, place)
            went.append(hop(m, 1, Z + k, mine, mine, across, f))
        return went

    def spread_core(m, went_x, diagonal):
        went = []
        for k in range(Z):
            if k:
                went_x[k - 1].wait_recv()
                mine = half_of(weights[m], zone(k) * 2 + y)
                went.append(hop(m, 3, k, mine, mine, sibling, f))
                diagonal[k - 1].wait_recv()
            mine = half_of(weights[m], zone(k) * 2 + 1 - y)
            went.append(hop(m, 3, Z + k, mine, mine, sibling, f))
        for copy in went:
            copy.wait_recv()
        own[m].wait()

    first_z = start_z(0)
    first_y = start_y(0)

    lanes = xs.shape[2]
    groups = ch // lanes

    @pl.loop(0, frames_n, step=64)
    def _(r):
        at = rows(r, 64)
        for j in range(groups):
            cols = pl.ds(j * lanes, lanes)
            xs[j, at, :] = frames[at, cols].astype(F32)
            ks[j, at, :] = keep[at, cols]

    def step(i, state):
        at = pl.ds(i, SEGS, stride=seg)
        new = []
        for j, (h, p) in enumerate(state):
            a = ks[j, at, :]
            h = a * h + (1.0 - a) * xs[j, at, :]
            p = p * a
            hs[j, at, :] = h
            ks[j, at, :] = p
            new.append((h, p))
        return tuple(new)

    nought = (jnp.zeros((SEGS, lanes), F32), jnp.ones((SEGS, lanes), F32))
    lax.fori_loop(0, seg, step, (nought,) * groups, unroll=4)
    before = []
    for j in range(groups):
        p, h = jnp.ones((1, lanes), F32), jnp.zeros((1, lanes), F32)
        before.append([])
        for s in range(SEGS):
            before[j].append((p, h))
            last = pl.ds((s + 1) * seg - 1, 1)
            p, h = ks[j, last, :] * p, ks[j, last, :] * h + hs[j, last, :]
        cols = pl.ds(j * lanes, lanes)
        ends[t, 0:8, cols] = jnp.broadcast_to(p, (8, lanes))
        ends[t, 8:16, cols] = jnp.broadcast_to(h, (8, lanes))
    states = [
        send(ends.at[t], ends.at[t], es.at[k], er.at[k], lax.rem(t + k, T), f)
        for k in range(1, T)
    ]
    first_x = spread_xy(0, first_z, first_y)
    second_z = start_z(1)
    second_y = start_y(1)
    for copy in states:
        copy.wait_recv()
    carried = jnp.zeros((1, ch), F32)
    for j in range(T):
        pj = ends[j, 0:1, :]
        hj = ends[j, 8:9, :]
        carried = jnp.where(j < t, pj * carried + hj, carried)
    for j in range(groups):
        cols = slice(j * lanes, (j + 1) * lanes)
        for s in range(SEGS):
            pb, hb = before[j][s]
            start = hb + pb * carried[:, cols]
            at = pl.ds(s * seg, seg)
            x1[at, ch + j * lanes : ch + (j + 1) * lanes] = (
                xs[j, at, :] - (hs[j, at, :] + ks[j, at, :] * start)
            ).astype(BF16)

    def neighbour(src, dst, n, tm):
        return pltpu.make_async_remote_copy(
            src_ref=src, dst_ref=dst, send_sem=ns.at[n], recv_sem=nr.at[n],
            device_id=(tm, f), device_id_type=MESH,
        )

    nxt, prv = lax.rem(t + 1, T), lax.rem(t + T - 1, T)
    has_next, has_prev = t < T - 1, t > 0

    tail = neighbour(x1.at[pl.ds(frames_n - lag, lag), pl.ds(ch, ch)], tail_in, 0, nxt)
    pl.when(has_next)(tail.start)
    x1[lag:, :ch] = x1[: frames_n - lag, ch:]

    first_diagonal = spread_diagonal(0, first_y)
    second_x = spread_xy(1, second_z, second_y)
    spread_core(0, first_x, first_diagonal)

    @pl.when(has_prev)
    def _():
        tail.wait_recv()
        x1[:lag, :ch] = tail_in[...]

    @pl.when(t == 0)
    def _():
        x1[:lag, :ch] = jnp.zeros((lag, ch), BF16)

    block = 128

    def blockwise(src, dst, ssems, rsems, tm):
        def copy(r):
            at = rows(r, block)
            return pltpu.make_async_remote_copy(
                src_ref=src.at[at, :], dst_ref=dst.at[at, :],
                send_sem=ssems.at[r // block], recv_sem=rsems.at[r // block],
                device_id=(tm, f), device_id_type=MESH,
            )

        return copy

    passed = blockwise(out1, prev_out, os, orr, nxt)
    back = blockwise(cb, cb_in, bs, br, prv)

    @pl.loop(0, frames_n, step=block)
    def _(r):
        at = rows(r, block)
        pre = jnp.dot(x1[at, :], w1[...], preferred_element_type=F32)
        th, sg = jnp.tanh(pre[:, :ch]), sigmoid(pre[:, ch:])
        th1[at, :] = th
        sg1[at, :] = sg
        out1[at, :] = (x1[at, ch:].astype(F32) + th * sg).astype(BF16)

        @pl.when(has_next)
        def _():
            passed(r).start()

    second_diagonal = spread_diagonal(1, second_y)

    @pl.when(t == 0)
    def _():
        prev_out[...] = jnp.zeros((frames_n, ch), BF16)

    spread_core(1, second_x, second_diagonal)

    @pl.loop(0, frames_n, step=block)
    def _(r):
        at = rows(r, block)

        @pl.when(has_prev)
        def _():
            passed(r).wait_recv()

        pre = jnp.dot(out1[at, :], w2[ch:, :], preferred_element_type=F32) + jnp.dot(
            prev_out[at, :], w2[:ch, :], preferred_element_type=F32
        )
        th, sg = jnp.tanh(pre[:, :ch]), sigmoid(pre[:, ch:])
        u = cot[at, :].astype(F32)
        top[at, :] = (out1[at, :].astype(F32) + th * sg).astype(BF16)
        g2 = jnp.concatenate(
            [u * sg * (1.0 - th * th), u * th * sg * (1.0 - sg)], axis=1
        ).astype(BF16)
        g[0, at, :] = g2
        cb[at, :] = lax.dot_general(
            g2, w2[:ch, :], (((1,), (1,)), ((), ())), preferred_element_type=F32
        ).astype(BF16)

        @pl.when(has_prev)
        def _():
            back(r).start()

    def partial(m, left, first_owner):
        @pl.loop(0, ch // shard)
        def _(j):
            cols = pl.ds(pl.multiple_of(j * shard, shard), shard)
            product = lax.dot_general(
                left[:, cols], g[m], (((0,), (0,)), ((), ())), preferred_element_type=F32
            )
            owner = first_owner + j
            part[m, owner // 2, owner % 2] = product.astype(BF16).reshape(2, 2, q, 2 * ch)

    two = Z // 2

    def span(h):
        return pl.ds(h * two, two)

    def core_phase(m, h):
        return send(part.at[m, span(h), :, 1 - c], core_in.at[m, span(h)],
                    ss.at[m, 0, h], sr.at[m, 0, h], sibling, f)

    def a_phase(m, h, copy):
        copy.wait_recv()
        for j in range(h * two, (h + 1) * two):
            for d in range(2):
                for e in range(2):
                    yy, xx = (d, e) if h == 0 else (e, d)
                    core_sum[m, d, j, e] = (
                        part[m, j, yy, c, xx].astype(F32) + core_in[m, j, yy, xx].astype(F32)
                    ).astype(BF16)
        mine, tm, fsdp = (y, t, over_y) if h == 0 else (x, across, f)
        return send(core_sum.at[m, 1 - mine, span(h)], a_in.at[m, span(h)],
                    ss.at[m, 1, h], sr.at[m, 1, h], tm, fsdp)

    def b_phase(m, h, copy):
        copy.wait_recv()
        mine = y if h == 0 else x
        for j in range(h * two, (h + 1) * two):
            for e in range(2):
                a_sum[m, e, j] = (
                    core_sum[m, mine, j, e].astype(F32) + a_in[m, j, e].astype(F32)
                ).astype(BF16)
        mine, tm, fsdp = (x, across, f) if h == 0 else (y, t, over_y)
        return send(a_sum.at[m, 1 - mine, span(h)], b_in.at[m, span(h)],
                    ss.at[m, 2, h], sr.at[m, 2, h], tm, fsdp)

    def z_copy(m, j, source):
        return pltpu.make_async_remote_copy(
            src_ref=b_sum.at[m, j], dst_ref=z_in.at[m, source],
            send_sem=zs.at[m, j], recv_sem=zr.at[m, source],
            device_id=(t, j * 2 + y), device_id_type=MESH,
        )

    def z_phase(m, h, copy):
        copy.wait_recv()
        mine = x if h == 0 else y
        for j in range(h * two, (h + 1) * two):
            b_sum[m, j] = (
                a_sum[m, mine, j].astype(F32) + b_in[m, j].astype(F32)
            ).astype(BF16)
            pl.when(z != j)(z_copy(m, j, z).start)

    def q_phase(m):
        total = b_sum[m, z].astype(F32)
        for k in range(1, Z):
            source = zone(k)
            z_copy(m, k, source).wait_recv()
            total += z_in[m, source].astype(F32)
        quarter[m, place] = total.astype(BF16)
        return [
            send(quarter.at[m, place], quarter.at[m, place], qs.at[m, k], qr.at[m, k],
                 lax.rem(t + k, T), f)
            for k in range(1, T)
        ]

    def finish(m, sends, grad):
        for copy in sends:
            copy.wait_recv()
        for j in range(T):
            grad[pl.ds(j * q, q), :] = quarter[m, j].astype(F32)

    half = ch // shard
    partial(0, prev_out, 0)
    core20 = core_phase(0, 0)
    partial(0, out1, half)
    core21 = core_phase(0, 1)
    a20 = a_phase(0, 0, core20)
    a21 = a_phase(0, 1, core21)

    @pl.loop(0, frames_n, step=block)
    def _(r):
        at = rows(r, block)
        pre2[at, :] = cot[at, :].astype(F32) + lax.dot_general(
            g[0, at, :], w2[ch:, :], (((1,), (1,)), ((), ())), preferred_element_type=F32
        )

    @pl.when(t == T - 1)
    def _():
        cb_in[...] = jnp.zeros((frames_n, ch), BF16)

    @pl.loop(0, frames_n, step=block)
    def _(r):
        at = rows(r, block)

        @pl.when(has_next)
        def _():
            back(r).wait_recv()

        u = pre2[at, :] + cb_in[at, :].astype(F32)
        th, sg = th1[at, :], sg1[at, :]
        g[1, at, :] = jnp.concatenate(
            [u * sg * (1.0 - th * th), u * th * sg * (1.0 - sg)], axis=1
        ).astype(BF16)

    partial(1, x1.at[:, pl.ds(0, ch)], 0)
    core10 = core_phase(1, 0)
    partial(1, x1.at[:, pl.ds(ch, ch)], half)
    core11 = core_phase(1, 1)
    a10 = a_phase(1, 0, core10)
    a11 = a_phase(1, 1, core11)
    b20 = b_phase(0, 0, a20)
    b21 = b_phase(0, 1, a21)
    b10 = b_phase(1, 0, a10)
    b11 = b_phase(1, 1, a11)
    z_phase(0, 0, b20)
    z_phase(0, 1, b21)
    z_phase(1, 0, b10)
    z_phase(1, 1, b11)
    last2 = q_phase(0)
    last1 = q_phase(1)
    finish(0, last2, grad2)
    finish(1, last1, grad1)

    for copy in pending:
        copy.wait_send()
    for m in range(2):
        for j in range(Z):
            pl.when(z != j)(z_copy(m, j, z).wait_send)
    pl.when(has_next)(tail.wait_send)
    for r in range(0, frames_n, block):
        pl.when(has_next)(passed(r).wait_send)
        pl.when(has_prev)(back(r).wait_send)


def fused(frames, retention, first_conv, second_conv, cotangent):
    _, n, ch = frames.shape
    shard, wide = first_conv.shape
    T, F, Z = 4, 8, 4
    q = shard // T
    vm = lambda shape, dtype: pltpu.VMEM(shape, dtype)
    dma = pltpu.SemaphoreType.DMA
    vspec = pl.BlockSpec(memory_space=pltpu.VMEM)
    anyspec = pl.BlockSpec(memory_space=pl.ANY)
    top, grad1, grad2 = pl.pallas_call(
        kernel,
        out_shape=(
            jax.ShapeDtypeStruct((n, ch), BF16),
            jax.ShapeDtypeStruct((shard, wide), F32),
            jax.ShapeDtypeStruct((shard, wide), F32),
        ),
        in_specs=[vspec, vspec, anyspec, anyspec, vspec],
        out_specs=(vspec, vspec, vspec),
        scratch_shapes=[
            vm((ch // 128, n, 128), F32), vm((ch // 128, n, 128), F32), vm((ch // 128, n, 128), F32),
            vm((n, wide), BF16), vm((n // 4, ch), BF16), vm((n, ch), BF16), vm((n, ch), BF16),
            vm((wide, wide), BF16), vm((wide, wide), BF16),
            vm((n, ch), F32), vm((n, ch), F32), vm((n, ch), F32),
            vm((2, n, wide), BF16), vm((n, ch), BF16), vm((n, ch), BF16),
            vm((T, 16, ch), F32),
            vm((2, Z, 2, 2, 2, q, wide), BF16), vm((2, Z, 2, 2, q, wide), BF16),
            vm((2, 2, Z, 2, q, wide), BF16), vm((2, Z, 2, q, wide), BF16),
            vm((2, 2, Z, q, wide), BF16), vm((2, Z, q, wide), BF16),
            vm((2, Z, q, wide), BF16), vm((2, Z, q, wide), BF16),
            vm((2, T, q, wide), BF16),
            dma((2,)), dma((2, 4, F)), dma((2, 4, F)), dma((T,)), dma((T,)),
            dma((1,)), dma((1,)), dma((4,)), dma((4,)), dma((4,)), dma((4,)),
            dma((2, 3, 2)), dma((2, 3, 2)), dma((2, Z)), dma((2, Z)),
            dma((2, T)), dma((2, T)),
        ],
        compiler_params=pltpu.CompilerParams(
            collective_id=0, has_side_effects=True, vmem_limit_bytes=56 * 2**20
        ),
        cost_estimate=pl.CostEstimate(
            flops=10 * n * wide * wide, bytes_accessed=8 * n * wide, transcendentals=2 * n * wide
        ),
    )(frames[0], retention[0], first_conv, second_conv, cotangent[0])
    return (top[None], grad1, grad2)


def solution(mesh):
    fits = mesh.shape["tm"] == 4 and mesh.shape["fsdp"] == 8
    in_specs = (
        P("fsdp", "tm", None),
        P("fsdp", "tm", None),
        P("fsdp", None),
        P("fsdp", None),
        P("fsdp", "tm", None),
    )
    out_specs = (P("fsdp", "tm", None), P("fsdp", None), P("fsdp", None))
    return jax.shard_map(
        fused if fits else on_device,
        mesh=mesh,
        in_specs=in_specs,
        out_specs=out_specs,
        check_vma=False,
    )
```
